256 devices in a mesh: ctx: 16 (over x, y_lo, core), dp: 16 (over y_hi, z).
Axes of the slice: x: 4, y: 4 (y_hi: 2, y_lo: 2; y = y_hi * 2 + y_lo), z: 8, core: 2. Of those that a mesh axis runs over, the one named last changes fastest.
Arguments:
- hidden_in: bfloat16 [16, 2048, 7168], P('dp', 'ctx'), may hold values from -6 to 6
- proj_weight: bfloat16 [7168, 576], P('ctx'), may hold values from -0.0625 to 0.0625
- proj_delta: bfloat16 [7168, 576], P('ctx'), may hold values from -0.03125 to 0.03125
- norm_gain: float32 [512], replicated, may hold values from 0.25 to 1.75
- queries: bfloat16 [16, 64, 73728], P('dp', 'ctx'), may hold values from -32 to 32
- out_grad: bfloat16 [16, 64, 65536], P('dp', 'ctx'), may hold values from -6 to 6
- seg_map: int32 [16, 16], P('dp'), may hold values from 0 to 15, each once within a row
Outputs:
- query_grad: bfloat16 [16, 64, 73728], P('dp', 'ctx')
- weight_grad: float32 [7168, 576], P('ctx')
The draws below stay inside these ranges and needn't reach their ends.
Inputs may be any that keep to these rules, and one draw needn't show every extreme that they name: Each row of seg_map names every segment 0 to 15 exactly once.
All inputs are finite; a program needn't handle non-finite values.
Results may differ from the reference program's by a relative error of at most 0.025.
The reference program's roundings to bfloat16 on the way count: a program that leaves them out, or rounds other values in their place, can miss the bound.
Values may be sent and summed in bfloat16 or wider, within the bound.
A program may use at most 128 MiB of HBM per device.

```python
import jax
import jax.numpy as jnp
from jax import lax

D = 7168
H = 128
LAT = 512
ROPE = 64
KD = 576
S_DEV = 128
Q_DEV = 4
STRIDE = 32
NSEQ = 16
S_LEN = 2048
QTOT = 64
N_CTX = 16


def draw_queries(key, part):
    key = jax.random.fold_in(key, 7)
    normal_key = jax.random.fold_in(key, 0)
    values = jnp.clip(jax.random.normal(normal_key, (NSEQ, QTOT, H * KD), jnp.float32), -4.0, 4.0)
    return values.astype(jnp.bfloat16)


def shard_levels(key, shape, pieces, low, largest):
    def one(dim, shards_of):
        draws = jax.random.uniform(jax.random.fold_in(jax.random.fold_in(key, 6), dim), (shards_of,), jnp.float32, low / len(pieces), largest / len(pieces))
        return jnp.repeat(jnp.exp(draws), shape[dim] // shards_of).reshape((-1,) + (1,) * (len(shape) - dim - 1))

    factor_of = one(*pieces[0])
    for cut in pieces[1:]:
        factor_of = factor_of * one(*cut)
    return factor_of


def noise(stream_key, dims, deviation, limit, cuts=(), kind=jnp.bfloat16):
    drawn = jax.random.normal(stream_key, dims, jnp.float32) * deviation
    if len(cuts) > 0:
        drawn = shard_levels(stream_key, dims, cuts, -0.22, 0.18) * drawn
    return jnp.clip(drawn, min=-limit, max=limit).astype(kind)


def setup_inputs(seed: int = 0) -> dict:
    key_list = jax.random.split(jax.random.key(seed), 8)
    hidden_in = noise(key_list[0], (NSEQ, S_LEN, D), 1.0, 6.0, ((0, 16), (1, 16)))
    proj_weight = noise(key_list[1], (D, KD), D ** -0.5, 0.0625, ((0, 16),))
    proj_delta = noise(key_list[2], (D, KD), (4 * D) ** -0.5, 0.03125, ((0, 16),))
    norm_gain = jnp.clip(1.0 + 0.15 * jax.random.normal(key_list[3], (LAT,), jnp.float32), 0.25, 1.75)
    queries = draw_queries(jax.random.fold_in(key_list[7], 71), 0)
    out_grad = noise(key_list[5], (NSEQ, QTOT, H * LAT), 1.0, 6.0, ((0, 16), (1, 16)))
    seg_map = jax.vmap(lambda own: jax.random.permutation(own, N_CTX))(jax.random.split(key_list[6], NSEQ)).reshape((NSEQ, N_CTX)).astype(jnp.int32)
    return dict(hidden_in=hidden_in, proj_weight=proj_weight, proj_delta=proj_delta, norm_gain=norm_gain, queries=queries, out_grad=out_grad, seg_map=seg_map)


NORM_EPS = 1e-06
SOFT_SCALE = 192.0 ** (-0.5)
ROPE_BASE = 10000.0

def rotary(positions):
    half_rope = ROPE // 2
    freqs = ROPE_BASE ** (-(jnp.arange(half_rope, dtype=jnp.float32) * 2.0 / ROPE))
    angles = positions.astype(jnp.float32)[:, None] * freqs[None, :]
    return (jnp.cos(angles), jnp.sin(angles))

def build_keys(projected, norm_gain, cosine, sine_table):
    half_rope = ROPE // 2
    latent = projected[:, :LAT]
    inverse = lax.rsqrt(lax.optimization_barrier(jnp.mean(latent * latent, axis=-1, keepdims=True)) + NORM_EPS)
    unit_latent = latent * inverse
    first_half = projected[:, LAT:LAT + half_rope]
    second_half = projected[:, LAT + half_rope:]
    key_rows = jnp.concatenate([unit_latent * norm_gain, first_half * cosine - second_half * sine_table, second_half * cosine + first_half * sine_table], axis=-1).astype(jnp.bfloat16)
    return (key_rows, unit_latent, inverse)

def keys_backward(grad_keys, norm_gain, unit_latent, inverse, cosine, sine_table):
    half_rope = ROPE // 2
    scaled = grad_keys[:, :LAT] * norm_gain
    grad_latent = inverse * (scaled - unit_latent * lax.optimization_barrier(jnp.mean(scaled * unit_latent, axis=-1, keepdims=True)))
    upper_half = grad_keys[:, LAT:LAT + half_rope]
    lower_half = grad_keys[:, LAT + half_rope:]
    return jnp.concatenate([grad_latent, upper_half * cosine + lower_half * sine_table, lower_half * cosine - upper_half * sine_table], axis=-1).astype(jnp.bfloat16)

def reference(hidden_in, proj_weight, proj_delta, norm_gain, queries, out_grad, seg_map):
    perturbed = (proj_weight.astype(jnp.float32) + proj_delta.astype(jnp.float32)).astype(jnp.bfloat16)

    def one_sequence(accum_grad, inputs):
        tokens, query_rows, grad_rows, segments = inputs
        key_pos = (segments[:, None] * S_DEV + jnp.arange(S_DEV, dtype=jnp.int32)[None, :]).reshape(-1)
        query_pos = (segments[:, None] * S_DEV + (jnp.arange(Q_DEV, dtype=jnp.int32)[None, :] + 1) * STRIDE - 1).reshape(-1)
        projected = jnp.dot(tokens, perturbed, preferred_element_type=jnp.float32)
        cosine, sine_table = rotary(key_pos)
        key_rows, unit_latent, inverse = build_keys(projected, norm_gain, cosine, sine_table)
        query_f = query_rows.reshape(QTOT, H, KD).astype(jnp.float32)
        key_f = key_rows.astype(jnp.float32)
        scores = SOFT_SCALE * jnp.einsum('qhc,kc->qhk', query_f, key_f)
        allowed = key_pos[None, None, :] <= query_pos[:, None, None]
        scores = jnp.where(allowed, scores, -jnp.inf)
        highest = lax.optimization_barrier(jnp.max(scores, axis=-1, keepdims=True))
        exponent = jnp.exp(scores - highest)
        probabilities = exponent / lax.optimization_barrier(jnp.sum(exponent, axis=-1, keepdims=True))
        weights = lax.optimization_barrier(probabilities.astype(jnp.bfloat16)).astype(jnp.float32)
        values = key_f[:, :LAT]
        outs = jnp.einsum('qhk,kc->qhc', weights, values)
        grad_out = grad_rows.reshape(QTOT, H, LAT).astype(jnp.float32)
        grad_probs = jnp.einsum('qhc,kc->qhk', grad_out, values)
        rowdot = lax.optimization_barrier(jnp.sum(grad_out * outs, axis=-1, keepdims=True))
        grad_scores = lax.optimization_barrier((SOFT_SCALE * probabilities * (grad_probs - rowdot)).astype(jnp.bfloat16)).astype(jnp.float32)
        grad_query = jnp.einsum('qhk,kc->qhc', grad_scores, key_f).astype(jnp.bfloat16).reshape(QTOT, H * KD)
        grad_keys = jnp.einsum('qhk,qhc->kc', grad_scores, query_f) + jnp.pad(jnp.einsum('qhk,qhc->kc', weights, grad_out), ((0, 0), (0, ROPE)))
        grad_projected = keys_backward(grad_keys, norm_gain, unit_latent, inverse, cosine, sine_table)

        def per_device(running, block_pair):
            rows_x, rows_g = block_pair
            dev_term = lax.dot_general(rows_x, rows_g, (((0,), (0,)), ((), ())), preferred_element_type=jnp.float32)
            dev_term = lax.optimization_barrier(dev_term.astype(jnp.bfloat16))
            return (running + dev_term.astype(jnp.float32), None)
        accum_grad, _ = lax.scan(per_device, accum_grad, (tokens.reshape(N_CTX, S_DEV, D), grad_projected.reshape(N_CTX, S_DEV, KD)))
        return (accum_grad, grad_query)
    weight_grad, query_grad = lax.scan(one_sequence, jnp.zeros((D, KD), jnp.float32), (hidden_in, queries, out_grad, seg_map))
    return (query_grad, weight_grad)
```

```python
import jax
import jax.numpy as jnp
from jax import lax
from jax.experimental import pallas as pl
from jax.experimental.pallas import tpu as pltpu
from jax.sharding import PartitionSpec as P

H = 128
LAT = 512
ROPE = 64
KD = LAT + ROPE
HALF = ROPE // 2
NORM_EPS = 1e-06
SOFT_SCALE = 192.0 ** (-0.5)
ROPE_BASE = 10000.0

NX, NY, NZ = 4, 2, 8
ROWS = 128
NQ = 4
QR = NQ * H
DSH = 448
CHIP = 2 * DSH
D = 16 * DSH
LT = LAT // 128
WF = DSH * KD // 128
KF = ROWS * KD // 128
ZF = 256
BF = jnp.bfloat16
F32 = jnp.float32
MESH = pl.DeviceIdType.MESH


def dot(a, b):
    return jnp.dot(a, b, preferred_element_type=F32)


def dot_t(a, b):
    return lax.dot_general(a, b, (((1,), (1,)), ((), ())), preferred_element_type=F32)


def t_dot(a, b):
    return lax.dot_general(a, b, (((0,), (0,)), ((), ())), preferred_element_type=F32)


def fold(part):
    n = part.shape[0] // 2
    return jnp.concatenate([part[:n], part[n:]], axis=1)


def unfold(part):
    return jnp.concatenate([part[:, :ROPE], part[:, ROPE:]], axis=0)


class Net:
    def __init__(self, send_sems, recv_sems):
        self.send_sems, self.recv_sems, self.all = send_sems, recv_sems, []

    def send(self, src, dst, to):
        i = len(self.all)
        copy = pltpu.make_async_remote_copy(
            src_ref=src,
            dst_ref=dst,
            send_sem=self.send_sems.at[i],
            recv_sem=self.recv_sems.at[i],
            device_id=to,
            device_id_type=MESH,
        )
        copy.start()
        self.all.append(copy)
        return copy


N_COPIES = 127


def kernel(
    seg, hid, w_ref, dw_ref, gain_ref, freq_ref, q_ref, g_ref,
    qg_ref, wg_ref,
    hid2, hidw, wbuf, acc, prec, unit_ref, inv_ref, trig,
    kflat, kbuf, e_ref, gp_ref, wt_ref, gs_ref, m_ref, l_ref, mj_ref, rd_ref,
    pf, pr, qacc,
    b1s, b1r, a1s, a1r, a2s, a2r, a3s, a3r, b2s, b2r, b3s, b3r, t_b,
    gflat, gbuf, hrecv, hsib, h_t, term,
    arflat, arz, ars, arr, agz,
    send_sems, recv_sems, local_sems,
):
    c, d = lax.axis_index("ctx"), lax.axis_index("dp")
    x, y, core = lax.div(c, 4), lax.rem(lax.div(c, 2), 2), lax.rem(c, 2)
    yh, z = lax.div(d, NZ), lax.rem(d, NZ)
    xr, xl, xo, yo = lax.rem(x + 1, 4), lax.rem(x + 3, 4), lax.rem(x + 2, 4), 1 - y
    sib = 1 - core

    def at(xx, yy, cc=core):
        return {"ctx": xx * 4 + yy * 2 + cc}

    right, left, across, twin = at(xr, y), at(xl, y), at(x, yo), at(x, y, sib)

    def chip(xx, yy):
        return xx * 2 + yy

    others = [(xr, y), (xl, y), (x, yo), (xo, y), (xr, yo), (xl, yo), (xo, yo)]
    zs = [lax.rem(z + k, NZ) for k in range(1, NZ)]

    barrier = pltpu.get_barrier_semaphore()
    peers = [at(*o) for o in others] + [twin]
    peers += [{"dp": yh * NZ + zz} for zz in zs] + [{"dp": (1 - yh) * NZ + z}]
    for peer in peers:
        pl.semaphore_signal(barrier, inc=1, device_id=peer, device_id_type=MESH)
    own_hidden = pltpu.make_async_copy(hid, hid2.at[pl.ds(0, ROWS)], local_sems.at[0])
    own_hidden.start()
    perturbed = (w_ref[...].astype(F32) + dw_ref[...].astype(F32)).astype(BF)
    mine = chip(x, y)
    for j in range(LT):
        wbuf[mine, pl.ds(DSH * j, DSH), :] = perturbed[:, 128 * j : 128 * j + 128]
    wbuf[mine, pl.ds(DSH * LT, DSH // 2), :] = fold(perturbed[:, LAT:])
    pl.semaphore_wait(barrier, len(peers))

    net = Net(send_sems, recv_sems)

    def all_gather(buf, slot, n_a, n_b, first, on_block):
        h_a, h_b = n_a // 2, n_b // 2

        def send(xx, yy, lo, n, to):
            ref = buf.at[slot(xx, yy), pl.ds(lo, n)]
            return net.send(ref, ref, to)

        a_r = send(x, y, 0, n_a, right)
        a_l = send(x, y, 0, n_a, left)
        b_y = send(x, y, n_a, n_b, across)
        b_r = send(x, y, n_a, n_b, right)
        b_l = send(x, y, n_a, n_b, left)
        a_y = send(x, y, 0, n_a, across)
        first()
        on_block(x, y)
        b_y.wait_recv()
        bp_r = send(x, yo, n_a, n_b, right)
        bp_l = send(x, yo, n_a, n_b, left)
        a_r.wait_recv()
        a_r2 = send(xl, y, 0, h_a, right)
        a_yl = send(xl, y, 0, n_a, across)
        a_l.wait_recv()
        a_l2 = send(xr, y, h_a, h_a, left)
        a_yr = send(xr, y, 0, n_a, across)
        b_r.wait_recv()
        b_r2 = send(xl, y, n_a, h_b, right)
        b_l.wait_recv()
        b_l2 = send(xr, y, n_a + h_b, h_b, left)
        on_block(xl, y)
        on_block(xr, y)
        a_y.wait_recv()
        on_block(x, yo)
        bp_r.wait_recv()
        bp_r2 = send(xl, yo, n_a, h_b, right)
        bp_l.wait_recv()
        bp_l2 = send(xr, yo, n_a + h_b, h_b, left)
        a_r2.wait_recv()
        a_y1 = send(xo, y, 0, h_a, across)
        a_l2.wait_recv()
        a_y2 = send(xo, y, h_a, h_a, across)
        a_yl.wait_recv()
        on_block(xl, yo)
        a_yr.wait_recv()
        on_block(xr, yo)
        b_r2.wait_recv()
        b_l2.wait_recv()
        on_block(xo, y)
        bp_r2.wait_recv()
        bp_l2.wait_recv()
        a_y1.wait_recv()
        a_y2.wait_recv()
        on_block(xo, yo)

    twin_hidden = net.send(hid, hid2.at[pl.ds(ROWS, ROWS)], twin)

    def after_weights_leave():
        pos = (seg[0, c] * ROWS + lax.broadcasted_iota(jnp.int32, (ROWS, HALF), 0)).astype(F32)
        angles = pos * freq_ref[...]
        trig[:, :HALF] = jnp.cos(angles)
        trig[:, HALF:] = jnp.sin(angles)
        acc[...] = jnp.zeros_like(acc)
        own_hidden.wait()
        twin_hidden.wait_recv()
        for i in range(NX * NY):
            hidw[:, 512 * i + DSH : 512 * i + 512] = jnp.zeros((2 * ROWS, 512 - DSH), BF)

        for cc in range(2):

            @pl.when(core == cc)
            def _():
                for i in range(NX * NY):
                    lo = CHIP * i + DSH * cc
                    hidw[:, 512 * i : 512 * i + DSH] = hid2[:, lo : lo + DSH]

    def project(xx, yy):
        p = chip(xx, yy)
        lhs = hidw[:, pl.ds(pl.multiple_of(p * 512, 512), DSH)]
        tiles = [wbuf[p, pl.ds(DSH * j, DSH), :] for j in range(LT)]
        for j in range(0, LT, 2):
            acc[:, 128 * j : 128 * j + 256] += dot(
                lhs, jnp.concatenate([tiles[j], tiles[j + 1]], axis=1)
            )
        acc[:, LAT:] += dot(lhs, unfold(wbuf[p, pl.ds(DSH * LT, DSH // 2), :]))

    all_gather(wbuf, chip, 864, 1152, after_weights_leave, project)
    swap = net.send(acc.at[pl.ds(ROWS, ROWS)], prec, twin)
    swap.wait_recv()
    projected = acc[:ROWS, :] + prec[...]

    latent = projected[:, :LAT]
    inverse = lax.rsqrt(jnp.mean(latent * latent, axis=-1, keepdims=True) + NORM_EPS)
    unit = latent * inverse
    unit_ref[...] = unit
    inv_ref[...] = jnp.broadcast_to(inverse, (ROWS, 128))
    key_latent = (unit * gain_ref[...]).astype(BF)
    cosine, sine = trig[:, :HALF], trig[:, HALF:]
    first_half, second_half = projected[:, LAT : LAT + HALF], projected[:, LAT + HALF :]
    key_rope = jnp.concatenate(
        [first_half * cosine - second_half * sine, second_half * cosine + first_half * sine],
        axis=-1,
    )
    for j in range(LT):
        kflat[c, pl.ds(ROWS * j, ROWS), :] = key_latent[:, 128 * j : 128 * j + 128]
    kflat[c, pl.ds(ROWS * LT, ROWS // 2), :] = fold(key_rope).astype(BF)

    def slot(xx, yy):
        return xx * 4 + yy * 2 + core

    def forwarding(buf, on_pair):
        waiting = []

        def pair():
            copy, xx, yy = waiting.pop(0)
            copy.wait_recv()
            on_pair(xx, yy)

        def on_block(xx, yy):
            ref = buf.at[slot(xx, yy)]
            waiting.append((net.send(ref, ref, twin), xx, yy))
            if len(waiting) > 1:
                pair()

        return on_block, pair

    def unpack(flat, rows, p):
        for cc in range(2):
            lo = pl.multiple_of(p * 256 + 128 * cc, 128)
            for j in range(LT):
                rows[pl.ds(lo, ROWS), 128 * j : 128 * j + 128] = flat[
                    2 * p + cc, pl.ds(ROWS * j, ROWS), :
                ]
            rows[pl.ds(lo, ROWS), LAT:] = unfold(flat[2 * p + cc, pl.ds(ROWS * LT, ROWS // 2), :])

    def chip_rows(p):
        return pl.ds(pl.multiple_of(p * 256, 256), 256)

    query_pos = (
        seg[0, c] * ROWS
        + (lax.div(lax.broadcasted_iota(jnp.int32, (1, QR), 1), H) + 1) * (ROWS // NQ)
        - 1
    )

    def start_scores():
        m_ref[...] = jnp.full_like(m_ref, -jnp.inf)
        l_ref[...] = jnp.zeros_like(l_ref)

    def scores(xx, yy):
        p = chip(xx, yy)
        unpack(kflat, kbuf, p)
        rows = chip_rows(p)
        row = lax.broadcasted_iota(jnp.int32, (256, 1), 0)
        key_pos = (
            jnp.where(row < ROWS, seg[0, 2 * p], seg[0, 2 * p + 1]) * ROWS + lax.rem(row, ROWS)
        )
        s = SOFT_SCALE * dot_t(kbuf[rows, :], q_ref[...])
        s = jnp.where(key_pos <= query_pos, s, -jnp.inf)
        old = m_ref[...]
        new = jnp.maximum(old, jnp.max(s, axis=0, keepdims=True))
        e = jnp.exp(s - new)
        e_ref[rows, :] = e
        m_ref[...] = new
        mj_ref[p] = new
        l_ref[...] = l_ref[...] * jnp.exp(old - new) + jnp.sum(e, axis=0, keepdims=True)
        gp_ref[rows, :] = dot_t(kbuf[rows, :LAT], g_ref[...])

    on_key, last_key = forwarding(kflat, scores)
    all_gather(kflat, slot, 256, 320, start_scores, on_key)

    parts = []
    for xx, yy in others:
        columns = pl.ds(pl.multiple_of(chip(xx, yy) * CHIP, 128), CHIP)
        parts.append(
            net.send(hid2.at[pl.ds(0, ROWS), columns], hrecv.at[chip(x, y)], at(xx, yy))
        )
    last_key()

    scale_by = 1.0 / l_ref[...]
    top = m_ref[...]
    rd_ref[...] = jnp.zeros_like(rd_ref)
    step = 64

    def weigh(i, _):
        rows = pl.ds(pl.multiple_of(i * step, step), step)
        factor = jnp.exp(mj_ref[lax.div(i, 256 // step)] - top) * scale_by
        weights = (e_ref[rows, :] * factor).astype(BF)
        wt_ref[rows, :] = weights
        rd_ref[...] += jnp.sum(weights.astype(F32) * gp_ref[rows, :], axis=0, keepdims=True)
        return 0

    lax.fori_loop(0, 2048 // step, weigh, 0)

    def key_gradient(xx, yy, i):
        p = chip(xx, yy)
        rows = chip_rows(p)
        factor = jnp.exp(mj_ref[p] - m_ref[...]) * (SOFT_SCALE / l_ref[...])
        gs = (e_ref[rows, :] * factor * (gp_ref[rows, :] - rd_ref[...])).astype(BF)
        gs_ref[rows, :] = gs
        lat = dot(gs, q_ref[:, :LAT]) + dot(wt_ref[rows, :], g_ref[...])
        rope = dot(gs, q_ref[:, LAT:])
        for cc in range(2):
            mine = slice(cc * ROWS, cc * ROWS + ROWS)
            for j in range(LT):
                pf[i, cc, pl.ds(ROWS * j, ROWS), :] = lat[mine, 128 * j : 128 * j + 128]
            pf[i, cc, pl.ds(ROWS * LT, ROWS // 2), :] = fold(rope[mine])
        return net.send(pf.at[i, sib], pr.at[i], twin)

    n_a, n_b = 256, 320
    h_a, h_b = n_a // 2, n_b // 2

    def summed(i, copy):
        copy.wait_recv()
        return pf[i, core] + pr[i]

    order = [(xo, yo), (xo, y), (xl, yo), (xr, yo), (x, yo), (xl, y), (xr, y), (x, y)]
    OO, OY, LO, RO, SO, LY, RY, SY = range(8)
    copies = [key_gradient(*order[0], 0), key_gradient(*order[1], 1)]
    sums = {}
    a1 = []
    b1 = []
    for i in range(8):
        if i + 2 < 8:
            copies.append(key_gradient(*order[i + 2], i + 2))
        block = summed(i, copies[i])
        pf[i, core] = block
        if i in (OO, OY):
            yi = 1 if i == OO else 0
            a1s[yi, 0] = block[:h_a].astype(BF)
            a1s[yi, 1] = block[h_a:n_a].astype(BF)
            a1.append(net.send(a1s.at[yi, 0], a1r.at[yi, 0], right))
            a1.append(net.send(a1s.at[yi, 1], a1r.at[yi, 1], left))
        if i in (OO, LO, RO, SO):
            bi = {OO: 0, LO: 1, RO: 2, SO: 3}[i]
            b1s[bi] = block[n_a:].astype(BF)
            b1.append(net.send(b1s.at[bi], b1r.at[bi], across))

    def own(i, lo, n):
        return pf[i, core, pl.ds(lo, n), :]

    qacc[...] = jnp.zeros_like(qacc)

    def query_gradient(first, last):
        def body(p, _):
            rows = chip_rows(p)
            qacc[...] += t_dot(gs_ref[rows, :], kbuf[rows, :])
            return 0

        lax.fori_loop(first, last, body, 0)

    b1[0].wait_recv()
    t_b[0] = own(OY, n_a, n_b) + b1r[0].astype(F32)
    b2s[0] = t_b[0, :h_b].astype(BF)
    b2s[1] = t_b[0, h_b:].astype(BF)
    b2 = [net.send(b2s.at[0], b2r.at[0], right), net.send(b2s.at[1], b2r.at[1], left)]
    for copy in a1:
        copy.wait_recv()
    a2 = []
    for yi, (il, ir) in enumerate(((LY, RY), (LO, RO))):
        a2s[yi, 0, :h_a] = (own(ir, 0, h_a) + a1r[yi, 0].astype(F32)).astype(BF)
        a2s[yi, 0, h_a:] = own(ir, h_a, h_a).astype(BF)
        a2s[yi, 1, :h_a] = own(il, 0, h_a).astype(BF)
        a2s[yi, 1, h_a:] = (own(il, h_a, h_a) + a1r[yi, 1].astype(F32)).astype(BF)
        a2.append(net.send(a2s.at[yi, 0], a2r.at[yi, 0], right))
        a2.append(net.send(a2s.at[yi, 1], a2r.at[yi, 1], left))
    query_gradient(0, 3)
    for copy in b1[1:]:
        copy.wait_recv()
    t_b[1] = own(LY, n_a, n_b) + b1r[1].astype(F32)
    t_b[2] = own(RY, n_a, n_b) + b1r[2].astype(F32)
    t_b[3] = own(SY, n_a, n_b) + b1r[3].astype(F32)
    for copy in b2:
        copy.wait_recv()
    b3s[0, :h_b] = (t_b[2, :h_b] + b2r[0].astype(F32)).astype(BF)
    b3s[0, h_b:] = t_b[2, h_b:].astype(BF)
    b3s[1, :h_b] = t_b[1, :h_b].astype(BF)
    b3s[1, h_b:] = (t_b[1, h_b:] + b2r[1].astype(F32)).astype(BF)
    b3 = [net.send(b3s.at[0], b3r.at[0], right), net.send(b3s.at[1], b3r.at[1], left)]
    for copy in a2:
        copy.wait_recv()
    a3s[...] = (own(SO, 0, n_a) + a2r[1, 0].astype(F32) + a2r[1, 1].astype(F32)).astype(BF)
    a3 = net.send(a3s, a3r, across)
    query_gradient(3, 6)
    for copy in b3:
        copy.wait_recv()
    grad_b = t_b[3] + b3r[0].astype(F32) + b3r[1].astype(F32)
    a3.wait_recv()
    grad_a = (
        own(SY, 0, n_a)
        + a2r[0, 0].astype(F32)
        + a2r[0, 1].astype(F32)
        + a3r[...].astype(F32)
    )

    grad_latent = jnp.concatenate(
        [grad_a[:ROWS], grad_a[ROWS:], grad_b[:ROWS], grad_b[ROWS : 2 * ROWS]], axis=1
    )
    grad_rope = unfold(grad_b[2 * ROWS :])
    unit = unit_ref[...]
    scaled = grad_latent * gain_ref[...]
    grad_latent = inv_ref[:, :1] * (
        scaled - unit * jnp.mean(scaled * unit, axis=-1, keepdims=True)
    )
    cosine, sine = trig[:, :HALF], trig[:, HALF:]
    upper, lower = grad_rope[:, :HALF], grad_rope[:, HALF:]
    grad_rope = jnp.concatenate(
        [upper * cosine + lower * sine, lower * cosine - upper * sine], axis=-1
    )
    for j in range(LT):
        gflat[c, pl.ds(ROWS * j, ROWS), :] = grad_latent[:, 128 * j : 128 * j + 128].astype(BF)
    gflat[c, pl.ds(ROWS * LT, ROWS // 2), :] = fold(grad_rope).astype(BF)

    def rest_of_query_gradient():
        query_gradient(6, 8)
        qg_ref[...] = qacc[...].astype(BF)
        hrecv[mine] = hid2[:ROWS, pl.ds(pl.multiple_of(mine * CHIP, 128), CHIP)]
        for copy in parts:
            copy.wait_recv()
        windows = []
        for p in range(NX * NY):
            window = pl.ds(pl.multiple_of(sib * 384, 128), 512)
            windows.append(net.send(hrecv.at[p, :, window], hsib.at[p], twin))
        for p in range(NX * NY):
            window = hrecv[p, :, pl.ds(pl.multiple_of(core * 384, 128), 512)]
            h_t[:, pl.ds(pl.multiple_of(256 * p + 128 * core, 128), 128)] = window.T
        for p in range(NX * NY):
            windows[p].wait_recv()
            h_t[:, pl.ds(pl.multiple_of(256 * p + 128 * sib, 128), 128)] = hsib[p].T
        term[...] = jnp.zeros_like(term)

    def add_term(xx, yy):
        p = chip(xx, yy)
        unpack(gflat, gbuf, p)
        term[...] += dot(h_t[:, chip_rows(p)], gbuf[chip_rows(p), :])

    on_grad, last_grad = forwarding(gflat, add_term)
    all_gather(gflat, slot, 256, 320, rest_of_query_gradient, on_grad)
    last_grad()

    valid = pl.ds(pl.multiple_of(core * 64, 64), DSH)
    for j in range(LT):
        arflat[pl.ds(DSH * j, DSH), :] = term[valid, 128 * j : 128 * j + 128].astype(BF)
    arflat[pl.ds(DSH * LT, DSH // 2), :] = fold(term[valid, LAT:]).astype(BF)
    arflat[pl.ds(WF, NZ * ZF - WF), :] = jnp.zeros((NZ * ZF - WF, 128), BF)

    def z_rows(zz):
        return pl.ds(pl.multiple_of(zz * ZF, ZF), ZF)

    to_z = [{"dp": yh * NZ + zz} for zz in zs]
    rs = [
        net.send(arflat.at[z_rows(zz)], arz.at[k], to)
        for k, (zz, to) in enumerate(zip(zs, to_z, strict=True))
    ]
    total = arflat[z_rows(z), :].astype(F32)
    for k, copy in enumerate(rs):
        copy.wait_recv()
        total += arz[k].astype(F32)
    ars[...] = total.astype(BF)
    half = net.send(ars, arr, {"dp": (1 - yh) * NZ + z})
    half.wait_recv()
    agz[z_rows(z), :] = (ars[...].astype(F32) + arr[...].astype(F32)).astype(BF)
    ag = [net.send(agz.at[z_rows(z)], agz.at[z_rows(z)], to) for to in to_z]
    for copy in ag:
        copy.wait_recv()
    for j in range(LT):
        wg_ref[:, 128 * j : 128 * j + 128] = agz[pl.ds(DSH * j, DSH), :].astype(F32)
    wg_ref[:, LAT:] = unfold(agz[pl.ds(DSH * LT, DSH // 2), :].astype(F32))

    for copy in net.all:
        copy.wait_send()
    assert len(net.all) == N_COPIES, len(net.all)


def on_device(hidden_in, proj_weight, proj_delta, norm_gain, queries, out_grad, seg_map):
    vmem = pl.BlockSpec(memory_space=pltpu.VMEM)
    half = jnp.arange(HALF, dtype=F32)
    freqs = ROPE_BASE ** (-(half * 2.0 / ROPE))
    v = pltpu.VMEM
    scratch = [
        v((2 * ROWS, D), BF), v((2 * ROWS, 8 * 512), BF), v((8, WF, 128), BF),
        v((2 * ROWS, KD), F32), v((ROWS, KD), F32), v((ROWS, LAT), F32), v((ROWS, 128), F32),
        v((ROWS, ROPE), F32),
        v((16, KF, 128), BF), v((2048, KD), BF), v((2048, QR), F32), v((2048, QR), F32),
        v((2048, QR), BF), v((2048, QR), BF), v((1, QR), F32), v((1, QR), F32),
        v((8, 1, QR), F32), v((1, QR), F32),
        v((8, 2, KF, 128), F32), v((8, KF, 128), F32), v((QR, KD), F32),
        v((4, 320, 128), BF), v((4, 320, 128), BF),
        v((2, 2, 128, 128), BF), v((2, 2, 128, 128), BF),
        v((2, 2, 256, 128), BF), v((2, 2, 256, 128), BF),
        v((256, 128), BF), v((256, 128), BF),
        v((2, 160, 128), BF), v((2, 160, 128), BF),
        v((2, 320, 128), BF), v((2, 320, 128), BF),
        v((4, 320, 128), F32),
        v((16, KF, 128), BF), v((2048, KD), BF),
        v((8, ROWS, CHIP), BF), v((8, ROWS, 512), BF), v((512, 2048), BF), v((512, KD), F32),
        v((NZ * ZF, 128), BF), v((7, ZF, 128), BF), v((ZF, 128), BF), v((ZF, 128), BF),
        v((NZ * ZF, 128), BF),
        pltpu.SemaphoreType.DMA((N_COPIES,)), pltpu.SemaphoreType.DMA((N_COPIES,)),
        pltpu.SemaphoreType.DMA((1,)),
    ]
    query_grad, weight_grad = pl.pallas_call(
        kernel,
        out_shape=(
            jax.ShapeDtypeStruct((QR, KD), BF),
            jax.ShapeDtypeStruct((DSH, KD), F32),
        ),
        in_specs=[
            pl.BlockSpec(memory_space=pltpu.SMEM),
            pl.BlockSpec(memory_space=pl.ANY),
        ]
        + [vmem] * 6,
        out_specs=(vmem, vmem),
        scratch_shapes=scratch,
        compiler_params=pltpu.CompilerParams(
            collective_id=0, has_side_effects=True, vmem_limit_bytes=60 * 2**20
        ),
        name="mla_backward",
    )(
        seg_map,
        hidden_in[0],
        proj_weight,
        proj_delta,
        norm_gain.reshape(1, LAT),
        freqs.reshape(1, HALF),
        queries[0].reshape(QR, KD),
        out_grad[0].reshape(QR, LAT),
    )
    return query_grad.reshape(1, NQ, H * KD), weight_grad


def solution(mesh):
    placed = (
        P("dp", "ctx", None),
        P("ctx", None),
        P("ctx", None),
        P(),
        P("dp", "ctx", None),
        P("dp", "ctx", None),
        P("dp", None),
    )
    return jax.shard_map(
        on_device,
        mesh=mesh,
        in_specs=placed,
        out_specs=(P("dp", "ctx", None), P("ctx", None)),
        check_vma=False,
    )
```

```python
import jax
import jax.numpy as jnp
import numpy as np
from jax import lax
from jax.experimental import pallas as pl
from jax.experimental.pallas import tpu as pltpu
from jax.sharding import PartitionSpec as P

H = 128
LAT = 512
ROPE = 64
KD = LAT + ROPE
HALF = ROPE // 2
NORM_EPS = 1e-06
SOFT_SCALE = 192.0 ** (-0.5)
ROPE_BASE = 10000.0

NX, NY, NZ = 4, 2, 8
ROWS = 128
NQ = 4
QR = NQ * H
DSH = 448
CHIP = 2 * DSH
D = 16 * DSH
LT = LAT // 128
WF = DSH * KD // 128
KF = ROWS * KD // 128
ZF = 128
W_ONE, W_A, W_B = 736, 544, 736
W_ODD = W_A + W_B
BF = jnp.bfloat16
F32 = jnp.float32
MESH = pl.DeviceIdType.MESH


def dot(a, b):
    return jnp.dot(a, b, preferred_element_type=F32)


def dot_t(a, b):
    return lax.dot_general(a, b, (((1,), (1,)), ((), ())), preferred_element_type=F32)


def t_dot(a, b):
    return lax.dot_general(a, b, (((0,), (0,)), ((), ())), preferred_element_type=F32)


def fold(part):
    n = part.shape[0] // 2
    return jnp.concatenate([part[:n], part[n:]], axis=1)


def unfold(part):
    return jnp.concatenate([part[:, :ROPE], part[:, ROPE:]], axis=0)


RING, KEYS, TWIN, ONCE = 0, 18, 36, 44
N_SEMS = ONCE + 41


class Net:
    def __init__(self, send_sems, recv_sems):
        self.send_sems, self.recv_sems = send_sems, recv_sems
        self.last, self.next = {}, {}

    def reuse(self, pool):
        self.next[pool] = 0

    def send(self, src, dst, to, pool=ONCE):
        i = pool + self.next.get(pool, 0)
        self.next[pool] = i + 1 - pool
        if i in self.last:
            self.last[i].wait_send()
        copy = pltpu.make_async_remote_copy(
            src_ref=src,
            dst_ref=dst,
            send_sem=self.send_sems.at[i],
            recv_sem=self.recv_sems.at[i],
            device_id=to,
            device_id_type=MESH,
        )
        copy.start()
        self.last[i] = copy
        return copy

    def finish(self):
        for i in sorted(self.last):
            self.last[i].wait_send()


def kernel(
    seg_in, hid, w_ref, dw_ref, gain_ref, freq_ref, q_in, g_in,
    qg_ref, wg_ref,
    seg, q_raw, g_raw, q_ref, g_ref, own_hid, hidw, hidt, wbuf, acc, prec, unit_ref, inv_ref, trig,
    kflat, kbuf, e_ref, gp_ref, wt_ref, gs_ref, m_ref, l_ref, mj_ref, rd_ref,
    pf, pb, pr, qacc,
    b1s, b1r, a1s, a1r, a2s, a2r, a3s, a3r, b2s, b2r, b3s, b3r, t_b,
    gflat, gbuf, hrecv, h_t, term, tsend, trecv,
    arflat, arz, agz,
    send_sems, recv_sems, local_sems,
):
    c, d = lax.axis_index("ctx"), lax.axis_index("dp")
    x, y, core = lax.div(c, 4), lax.rem(lax.div(c, 2), 2), lax.rem(c, 2)
    yh, z = lax.div(d, NZ), lax.rem(d, NZ)
    xr, xl, xo, yo = lax.rem(x + 1, 4), lax.rem(x + 3, 4), lax.rem(x + 2, 4), 1 - y
    sib = 1 - core

    def at(xx, yy, cc=core):
        return {"ctx": xx * 4 + yy * 2 + cc}

    right, left, across, twin = at(xr, y), at(xl, y), at(x, yo), at(x, y, sib)

    def chip(xx, yy):
        return xx * 2 + yy

    others = [(xr, y), (xl, y), (x, yo), (xo, y), (xr, yo), (xl, yo), (xo, yo)]
    senders = [(xl, y), (xr, y), (x, yo), (xo, y), (xl, yo), (xr, yo), (xo, yo)]
    z_up = {"dp": yh * NZ + lax.rem(z + 1, NZ)}
    z_down = {"dp": yh * NZ + lax.rem(z + NZ - 1, NZ)}
    sequences = [
        lax.rem(yh + k // NZ, 2) * NZ + lax.rem(z + k % NZ, NZ) for k in range(1, 2 * NZ)
    ]

    barrier = pltpu.get_barrier_semaphore()
    peers = [right, left, across, twin] + [{"dp": dd} for dd in sequences]
    for peer in peers:
        pl.semaphore_signal(barrier, inc=1, device_id=peer, device_id_type=MESH)
    own_hidden = pltpu.make_async_copy(hid, own_hid, local_sems.at[0])
    own_hidden.start()
    own_queries = pltpu.make_async_copy(q_in, q_raw, local_sems.at[1])
    own_queries.start()
    own_grads = pltpu.make_async_copy(g_in, g_raw, local_sems.at[2])
    own_grads.start()
    own_segments = pltpu.make_async_copy(seg_in, seg, local_sems.at[3])
    own_segments.start()
    perturbed = (w_ref[...].astype(F32) + dw_ref[...].astype(F32)).astype(BF)
    mine = chip(x, y)
    for j in range(LT):
        wbuf[mine, pl.ds(DSH * j, DSH), :] = perturbed[:, 128 * j : 128 * j + 128]
    wbuf[mine, pl.ds(DSH * LT, DSH // 2), :] = fold(perturbed[:, LAT:])
    pl.semaphore_wait(barrier, len(peers))

    net = Net(send_sems, recv_sems)

    def all_gather(pool, buf, slot, base, n_a, n_b, idle, on_block):
        h_a, h_b = n_a // 2, n_b // 2

        def send(xx, yy, lo, n, to):
            ref = buf.at[slot(xx, yy), pl.ds(pl.multiple_of(base + lo, 16), n)]
            return net.send(ref, ref, to, pool)

        a_r = send(x, y, 0, n_a, right)
        a_l = send(x, y, 0, n_a, left)
        b_y = send(x, y, n_a, n_b, across)
        b_r = send(x, y, n_a, n_b, right)
        b_l = send(x, y, n_a, n_b, left)
        a_y = send(x, y, 0, n_a, across)
        idle[0]()
        on_block(x, y)
        b_y.wait_recv()
        bp_r = send(x, yo, n_a, n_b, right)
        bp_l = send(x, yo, n_a, n_b, left)
        a_r.wait_recv()
        a_r2 = send(xl, y, 0, h_a, right)
        a_yl = send(xl, y, 0, n_a, across)
        a_l.wait_recv()
        a_l2 = send(xr, y, h_a, h_a, left)
        a_yr = send(xr, y, 0, n_a, across)
        b_r.wait_recv()
        b_r2 = send(xl, y, n_a, h_b, right)
        b_l.wait_recv()
        b_l2 = send(xr, y, n_a + h_b, h_b, left)
        idle[1]()
        on_block(xl, y)
        on_block(xr, y)
        a_y.wait_recv()
        on_block(x, yo)
        bp_r.wait_recv()
        bp_r2 = send(xl, yo, n_a, h_b, right)
        bp_l.wait_recv()
        bp_l2 = send(xr, yo, n_a + h_b, h_b, left)
        a_r2.wait_recv()
        a_y1 = send(xo, y, 0, h_a, across)
        a_l2.wait_recv()
        a_y2 = send(xo, y, h_a, h_a, across)
        idle[2]()
        a_yl.wait_recv()
        on_block(xl, yo)
        a_yr.wait_recv()
        on_block(xr, yo)
        b_r2.wait_recv()
        b_l2.wait_recv()
        on_block(xo, y)
        bp_r2.wait_recv()
        bp_l2.wait_recv()
        a_y1.wait_recv()
        a_y2.wait_recv()
        on_block(xo, yo)

    def nothing():
        pass

    def angles():
        pos = (seg[0, c] * ROWS + lax.broadcasted_iota(jnp.int32, (ROWS, HALF), 0)).astype(F32)
        angle = pos * freq_ref[...]
        trig[:, :HALF] = jnp.cos(angle)
        trig[:, HALF:] = jnp.sin(angle)
        acc[...] = jnp.zeros_like(acc)

    def heads_to_rows(src, dst, width):
        def body(i, _):
            pieces = []
            for k in range(2):
                lo = pl.multiple_of((2 * i + k) * 2 * width, 128)
                block = src[:, pl.ds(lo, 2 * width)].astype(F32)
                pieces += [block[:, :width], block[:, width:]]
            rows = pl.ds(pl.multiple_of(i * 16, 16), 16)
            dst[rows, :] = jnp.concatenate(pieces, axis=0).astype(BF)
            return 0

        lax.fori_loop(0, QR // 16, body, 0)

    def hidden_windows():
        own_segments.wait()
        angles()
        own_hidden.wait()
        for i in range(NX * NY):
            pad = slice(512 * i + DSH, 512 * i + 512)
            hidw[:ROWS, pad] = jnp.zeros((ROWS, 512 - DSH), BF)
            hidt[:, pad] = jnp.zeros((ROWS, 512 - DSH), BF)

        for cc in range(2):

            @pl.when(core == cc)
            def _():
                for i in range(NX * NY):
                    lo, other = CHIP * i + DSH * cc, CHIP * i + DSH * (1 - cc)
                    hidw[:ROWS, 512 * i : 512 * i + DSH] = own_hid[:, lo : lo + DSH]
                    hidt[:, 512 * i : 512 * i + DSH] = own_hid[:, other : other + DSH]

        twin_hidden.append(net.send(hidt, hidw.at[pl.ds(ROWS, ROWS)], twin))
        hrecv[mine] = own_hid[:, pl.ds(pl.multiple_of(mine * CHIP, 128), CHIP)]

    twin_hidden = []

    def query_rows():
        own_queries.wait()
        heads_to_rows(q_raw, q_ref, KD)

    def grad_rows():
        for i in range(4):
            to_chip(i)
        own_grads.wait()
        heads_to_rows(g_raw, g_ref, LAT)

    def project(xx, yy):
        p = chip(xx, yy)
        lhs = hidw[:, pl.ds(pl.multiple_of(p * 512, 512), DSH)]
        tiles = [wbuf[p, pl.ds(DSH * j, DSH), :] for j in range(LT)]
        for j in range(0, LT, 2):
            acc[:, 128 * j : 128 * j + 256] += dot(
                lhs, jnp.concatenate([tiles[j], tiles[j + 1]], axis=1)
            )
        acc[:, LAT:] += dot(lhs, unfold(wbuf[p, pl.ds(DSH * LT, DSH // 2), :]))

    odd = lax.rem(z, 2)
    from_z = []
    parts = []

    def to_chip(k):
        xx, yy = others[k]
        columns = pl.ds(pl.multiple_of(chip(xx, yy) * CHIP, 128), CHIP)
        parts.append(net.send(own_hid.at[:, columns], hrecv.at[mine], at(xx, yy)))

    def project_next():
        xx, yy, copies = from_z.pop(0)
        for copy in copies:
            copy.wait_recv()
        project(xx, yy)

    def on_weights(xx, yy):
        def send(lo, n, to):
            ref = wbuf.at[chip(xx, yy), pl.ds(pl.multiple_of(odd * W_ODD + lo, 16), n)]
            return net.send(ref, ref, to)

        k = n_blocks[0]
        n_blocks[0] += 1
        if k == 0:
            copies = []
        elif k == 7:
            copies = [send(0, W_ONE // 2, z_up), send(W_ONE // 2, W_ONE // 2, z_down)]
        else:
            copies = [send(0, W_ONE, z_up if k in (1, 3, 4) else z_down)]
        from_z.append((xx, yy, copies))
        if k == 4:
            twin_hidden[0].wait_recv()
        if k >= 4:
            project_next()
        if k == 7:
            while from_z:
                project_next()

    n_blocks = [0]
    idle = (hidden_windows, query_rows, grad_rows)
    all_gather(RING, wbuf, chip, odd * W_ONE, W_A, W_B, idle, on_weights)
    swap = net.send(acc.at[pl.ds(ROWS, ROWS)], prec, twin)
    swap.wait_recv()
    projected = acc[:ROWS, :] + prec[...]

    latent = projected[:, :LAT]
    inverse = lax.rsqrt(jnp.mean(latent * latent, axis=-1, keepdims=True) + NORM_EPS)
    unit = latent * inverse
    unit_ref[...] = unit
    inv_ref[...] = jnp.broadcast_to(inverse, (ROWS, 128))
    key_latent = (unit * gain_ref[...]).astype(BF)
    cosine, sine = trig[:, :HALF], trig[:, HALF:]
    first_half, second_half = projected[:, LAT : LAT + HALF], projected[:, LAT + HALF :]
    key_rope = jnp.concatenate(
        [first_half * cosine - second_half * sine, second_half * cosine + first_half * sine],
        axis=-1,
    )
    for j in range(LT):
        kflat[c, pl.ds(ROWS * j, ROWS), :] = key_latent[:, 128 * j : 128 * j + 128]
    kflat[c, pl.ds(ROWS * LT, ROWS // 2), :] = fold(key_rope).astype(BF)

    def slot(xx, yy):
        return xx * 4 + yy * 2 + core

    waiting = []

    def pair():
        copy, xx, yy = waiting.pop(0)
        copy.wait_recv()
        scores(xx, yy)

    def on_key(xx, yy):
        ref = kflat.at[slot(xx, yy)]
        waiting.append((net.send(ref, ref, twin, TWIN), xx, yy))
        if len(waiting) > 1:
            pair()

    def unpack(flat, rows, lo):
        for j in range(LT):
            rows[pl.ds(lo, ROWS), 128 * j : 128 * j + 128] = flat[pl.ds(ROWS * j, ROWS), :]
        rows[pl.ds(lo, ROWS), LAT:] = unfold(flat[pl.ds(ROWS * LT, ROWS // 2), :])

    def chip_rows(p):
        return pl.ds(pl.multiple_of(p * 256, 256), 256)

    query_pos = (
        seg[0, c] * ROWS
        + (lax.rem(lax.broadcasted_iota(jnp.int32, (1, QR), 1), NQ) + 1) * (ROWS // NQ)
        - 1
    )

    def start_scores():
        m_ref[...] = jnp.full_like(m_ref, -jnp.inf)
        l_ref[...] = jnp.zeros_like(l_ref)

    def scores(xx, yy):
        p = chip(xx, yy)
        for cc in range(2):
            unpack(kflat.at[2 * p + cc], kbuf, pl.multiple_of(p * 256 + 128 * cc, 128))
        rows = chip_rows(p)
        row = lax.broadcasted_iota(jnp.int32, (256, 1), 0)
        key_pos = (
            jnp.where(row < ROWS, seg[0, 2 * p], seg[0, 2 * p + 1]) * ROWS + lax.rem(row, ROWS)
        )
        s = SOFT_SCALE * dot_t(kbuf[rows, :], q_ref[...])
        s = jnp.where(key_pos <= query_pos, s, -jnp.inf)
        old = m_ref[...]
        new = jnp.maximum(old, jnp.max(s, axis=0, keepdims=True))
        e = jnp.exp(s - new)
        e_ref[rows, :] = e
        m_ref[...] = new
        mj_ref[p] = new
        l_ref[...] = l_ref[...] * jnp.exp(old - new) + jnp.sum(e, axis=0, keepdims=True)
        gp_ref[rows, :] = dot_t(kbuf[rows, :LAT], g_ref[...])

    all_gather(KEYS, kflat, slot, 0, 256, 320, (start_scores, nothing, nothing), on_key)

    for k in range(4, 7):
        to_chip(k)
    pair()

    scale_by = 1.0 / l_ref[...]
    top = m_ref[...]
    rd_ref[...] = jnp.zeros_like(rd_ref)
    step = 64

    def weigh(i, _):
        rows = pl.ds(pl.multiple_of(i * step, step), step)
        factor = jnp.exp(mj_ref[lax.div(i, 256 // step)] - top) * scale_by
        weights = (e_ref[rows, :] * factor).astype(BF)
        wt_ref[rows, :] = weights
        rd_ref[...] += jnp.sum(weights.astype(F32) * gp_ref[rows, :], axis=0, keepdims=True)
        return 0

    lax.fori_loop(0, 2048 // step, weigh, 0)

    arrivals = [(x, y), (xl, y), (xr, y), (x, yo), (xl, yo), (xr, yo), (xo, y), (xo, yo)]

    def turn(i):
        if i > 0:
            parts[(0, 1, 2, 4, 5, 3, 6)[i - 1]].wait_recv()
        h_t[:, 128 * i : 128 * i + 128] = hrecv[chip(*arrivals[i])].T

    def key_gradient(xx, yy, i):
        p = chip(xx, yy)
        rows = chip_rows(p)
        factor = jnp.exp(mj_ref[p] - m_ref[...]) * (SOFT_SCALE / l_ref[...])
        gs = (e_ref[rows, :] * factor * (gp_ref[rows, :] - rd_ref[...])).astype(BF)
        gs_ref[rows, :] = gs
        lat = dot(gs, q_ref[:, :LAT]) + dot(wt_ref[rows, :], g_ref[...])
        rope = dot(gs, q_ref[:, LAT:])
        for cc in range(2):
            half = slice(cc * ROWS, cc * ROWS + ROWS)
            for j in range(LT):
                tile = lat[half, 128 * j : 128 * j + 128]
                pf[i, cc, pl.ds(ROWS * j, ROWS), :] = tile
                pb[i, cc, pl.ds(ROWS * j, ROWS), :] = tile.astype(BF)
            tile = fold(rope[half])
            pf[i, cc, pl.ds(ROWS * LT, ROWS // 2), :] = tile
            pb[i, cc, pl.ds(ROWS * LT, ROWS // 2), :] = tile.astype(BF)
        return net.send(pb.at[i, sib], pr.at[i], twin)

    n_a, n_b = 256, 320
    h_a, h_b = n_a // 2, n_b // 2

    def summed(i, copy):
        copy.wait_recv()
        return pf[i, core] + pr[i].astype(F32)

    order = [(xo, yo), (xo, y), (xl, yo), (xr, yo), (x, yo), (xl, y), (xr, y), (x, y)]
    OO, OY, LO, RO, SO, LY, RY, SY = range(8)
    copies = [key_gradient(*order[0], 0), key_gradient(*order[1], 1)]
    net.reuse(RING)
    sums = {}
    a1 = []
    b1 = []
    for i in range(8):
        if i + 2 < 8:
            copies.append(key_gradient(*order[i + 2], i + 2))
        block = summed(i, copies[i])
        pf[i, core] = block
        if i in (OO, OY):
            yi = 1 if i == OO else 0
            a1s[yi, 0] = block[:h_a].astype(BF)
            a1s[yi, 1] = block[h_a:n_a].astype(BF)
            a1.append(net.send(a1s.at[yi, 0], a1r.at[yi, 0], right, RING))
            a1.append(net.send(a1s.at[yi, 1], a1r.at[yi, 1], left, RING))
        if i in (OO, LO, RO, SO):
            bi = {OO: 0, LO: 1, RO: 2, SO: 3}[i]
            b1s[bi] = block[n_a:].astype(BF)
            b1.append(net.send(b1s.at[bi], b1r.at[bi], across, RING))

    def own(i, lo, n):
        return pf[i, core, pl.ds(lo, n), :]

    def query_gradient():
        qacc[...] = jnp.zeros_like(qacc)

        def body(p, _):
            rows = chip_rows(p)
            qacc[...] += t_dot(gs_ref[rows, :], kbuf[rows, :])
            return 0

        lax.fori_loop(0, NX * NY, body, 0)

    def rows_to_heads():
        def body(i, _):
            rows = qacc[pl.ds(pl.multiple_of(i * 16, 16), 16), :]
            heads = jnp.concatenate([rows[4 * k : 4 * k + 4] for k in range(4)], axis=1)
            qg_ref[:, pl.ds(pl.multiple_of(i * 4 * KD, 128), 4 * KD)] = heads.astype(BF)
            return 0

        lax.fori_loop(0, QR // 16, body, 0)

    b1[0].wait_recv()
    t_b[0] = own(OY, n_a, n_b) + b1r[0].astype(F32)
    b2s[0] = t_b[0, :h_b].astype(BF)
    b2s[1] = t_b[0, h_b:].astype(BF)
    b2 = [net.send(b2s.at[0], b2r.at[0], right, RING), net.send(b2s.at[1], b2r.at[1], left, RING)]
    for copy in a1:
        copy.wait_recv()
    a2 = []
    for yi, (il, ir) in enumerate(((LY, RY), (LO, RO))):
        a2s[yi, 0, :h_a] = (own(ir, 0, h_a) + a1r[yi, 0].astype(F32)).astype(BF)
        a2s[yi, 0, h_a:] = own(ir, h_a, h_a).astype(BF)
        a2s[yi, 1, :h_a] = own(il, 0, h_a).astype(BF)
        a2s[yi, 1, h_a:] = (own(il, h_a, h_a) + a1r[yi, 1].astype(F32)).astype(BF)
        a2.append(net.send(a2s.at[yi, 0], a2r.at[yi, 0], right, RING))
        a2.append(net.send(a2s.at[yi, 1], a2r.at[yi, 1], left, RING))
    for i in (0, 1, 2, 3, 6):
        turn(i)
    for copy in b1[1:]:
        copy.wait_recv()
    t_b[1] = own(LY, n_a, n_b) + b1r[1].astype(F32)
    t_b[2] = own(RY, n_a, n_b) + b1r[2].astype(F32)
    t_b[3] = own(SY, n_a, n_b) + b1r[3].astype(F32)
    for copy in b2:
        copy.wait_recv()
    b3s[0, :h_b] = (t_b[2, :h_b] + b2r[0].astype(F32)).astype(BF)
    b3s[0, h_b:] = t_b[2, h_b:].astype(BF)
    b3s[1, :h_b] = t_b[1, :h_b].astype(BF)
    b3s[1, h_b:] = (t_b[1, h_b:] + b2r[1].astype(F32)).astype(BF)
    b3 = [net.send(b3s.at[0], b3r.at[0], right, RING), net.send(b3s.at[1], b3r.at[1], left, RING)]
    for copy in a2:
        copy.wait_recv()
    a3s[...] = (own(SO, 0, n_a) + a2r[1, 0].astype(F32) + a2r[1, 1].astype(F32)).astype(BF)
    a3 = net.send(a3s, a3r, across, RING)
    for copy in b3:
        copy.wait_recv()
    grad_b = t_b[3] + b3r[0].astype(F32) + b3r[1].astype(F32)
    a3.wait_recv()
    grad_a = (
        own(SY, 0, n_a)
        + a2r[0, 0].astype(F32)
        + a2r[0, 1].astype(F32)
        + a3r[...].astype(F32)
    )

    grad_latent = jnp.concatenate(
        [grad_a[:ROWS], grad_a[ROWS:], grad_b[:ROWS], grad_b[ROWS : 2 * ROWS]], axis=1
    )
    grad_rope = unfold(grad_b[2 * ROWS :])
    unit = unit_ref[...]
    scaled = grad_latent * gain_ref[...]
    grad_latent = inv_ref[:, :1] * (
        scaled - unit * jnp.mean(scaled * unit, axis=-1, keepdims=True)
    )
    cosine, sine = trig[:, :HALF], trig[:, HALF:]
    upper, lower = grad_rope[:, :HALF], grad_rope[:, HALF:]
    grad_rope = jnp.concatenate(
        [upper * cosine + lower * sine, lower * cosine - upper * sine], axis=-1
    )
    for j in range(LT):
        gflat[c, pl.ds(ROWS * j, ROWS), :] = grad_latent[:, 128 * j : 128 * j + 128].astype(BF)
    gflat[c, pl.ds(ROWS * LT, ROWS // 2), :] = fold(grad_rope).astype(BF)

    blocks = []

    def add_term(xx, yy):
        k = len(blocks)
        blocks.append(k)
        if k in (4, 5, 7):
            turn(k)
        unpack(gflat.at[slot(xx, yy)], gbuf, 128 * k)
        if k == 1:
            term[...] = dot(h_t[:, :256], gbuf[:256, :])
        elif k % 2:
            two = slice(128 * k - 128, 128 * k + 128)
            term[...] += dot(h_t[:, two], gbuf[two, :])

    net.reuse(KEYS)
    all_gather(KEYS, gflat, slot, 0, 256, 320, (nothing, nothing, nothing), add_term)

    def pack(dst, first):
        rows = pl.ds(pl.multiple_of(first, 64), DSH)
        for j in range(LT):
            dst[pl.ds(DSH * j, DSH), :] = term[rows, 128 * j : 128 * j + 128].astype(BF)
        dst[pl.ds(DSH * LT, DSH // 2), :] = fold(term[rows, LAT:]).astype(BF)

    pack(tsend, sib * DSH)
    swap = net.send(tsend, trecv, twin)

    rows = pl.ds(pl.multiple_of(core * DSH, 64), DSH)
    swap.wait_recv()
    for j in range(LT):
        tile = pl.ds(DSH * j, DSH)
        arflat[tile, :] = (term[rows, 128 * j : 128 * j + 128] + trecv[tile, :].astype(F32)).astype(
            BF
        )
    tile = pl.ds(DSH * LT, DSH // 2)
    arflat[tile, :] = (fold(term[rows, LAT:]) + trecv[tile, :].astype(F32)).astype(BF)
    arflat[pl.ds(WF, 16 * ZF - WF), :] = jnp.zeros((16 * ZF - WF, 128), BF)

    def part_of(dd):
        return pl.ds(pl.multiple_of(dd * ZF, ZF), ZF)

    sums_in = [
        net.send(arflat.at[part_of(dd)], arz.at[k], {"dp": dd}) for k, dd in enumerate(sequences)
    ]
    query_gradient()
    total = arflat[part_of(d), :].astype(F32)
    for k, copy in enumerate(sums_in):
        copy.wait_recv()
        total += arz[k].astype(F32)
    agz[part_of(d), :] = total.astype(BF)
    net.reuse(RING)
    sums_out = [
        net.send(agz.at[part_of(d)], agz.at[part_of(d)], {"dp": dd}, RING) for dd in sequences
    ]
    rows_to_heads()
    for copy in sums_out:
        copy.wait_recv()
    for j in range(LT):
        wg_ref[:, 128 * j : 128 * j + 128] = agz[pl.ds(DSH * j, DSH), :].astype(F32)
    wg_ref[:, LAT:] = unfold(agz[pl.ds(DSH * LT, DSH // 2), :].astype(F32))

    net.finish()
    assert len(net.last) == N_SEMS, len(net.last)


def on_device(hidden_in, proj_weight, proj_delta, norm_gain, queries, out_grad, seg_map):
    vmem = pl.BlockSpec(memory_space=pltpu.VMEM)
    freqs = np.float32(ROPE_BASE) ** (-(np.arange(HALF, dtype=np.float32) * 2 / ROPE))
    v = pltpu.VMEM
    scratch = [
        pltpu.SMEM((1, 16), jnp.int32),
        v((NQ, H * KD), BF), v((NQ, H * LAT), BF), v((QR, KD), BF), v((QR, LAT), BF),
        v((ROWS, D), BF), v((2 * ROWS, 8 * 512), BF), v((ROWS, 8 * 512), BF), v((8, WF, 128), BF),
        v((2 * ROWS, KD), F32), v((ROWS, KD), F32), v((ROWS, LAT), F32), v((ROWS, 128), F32),
        v((ROWS, ROPE), F32),
        v((16, KF, 128), BF), v((2048, KD), BF), v((2048, QR), F32), v((2048, QR), F32),
        v((2048, QR), BF), v((2048, QR), BF), v((1, QR), F32), v((1, QR), F32),
        v((8, 1, QR), F32), v((1, QR), F32),
        v((8, 2, KF, 128), F32), v((8, 2, KF, 128), BF), v((8, KF, 128), BF), v((QR, KD), F32),
        v((4, 320, 128), BF), v((4, 320, 128), BF),
        v((2, 2, 128, 128), BF), v((2, 2, 128, 128), BF),
        v((2, 2, 256, 128), BF), v((2, 2, 256, 128), BF),
        v((256, 128), BF), v((256, 128), BF),
        v((2, 160, 128), BF), v((2, 160, 128), BF),
        v((2, 320, 128), BF), v((2, 320, 128), BF),
        v((4, 320, 128), F32),
        v((16, KF, 128), BF), v((1024, KD), BF),
        v((8, ROWS, CHIP), BF), v((CHIP, 1024), BF), v((CHIP, KD), F32),
        v((WF, 128), BF), v((WF, 128), BF),
        v((16 * ZF, 128), BF), v((15, ZF, 128), BF), v((16 * ZF, 128), BF),
        pltpu.SemaphoreType.DMA((N_SEMS,)), pltpu.SemaphoreType.DMA((N_SEMS,)),
        pltpu.SemaphoreType.DMA((4,)),
    ]
    query_grad, weight_grad = pl.pallas_call(
        kernel,
        out_shape=(
            jax.ShapeDtypeStruct((NQ, H * KD), BF),
            jax.ShapeDtypeStruct((DSH, KD), F32),
        ),
        in_specs=[
            pl.BlockSpec(memory_space=pl.ANY),
            pl.BlockSpec(memory_space=pl.ANY),
        ]
        + [vmem] * 4
        + [pl.BlockSpec(memory_space=pl.ANY)] * 2,
        out_specs=(vmem, vmem),
        scratch_shapes=scratch,
        compiler_params=pltpu.CompilerParams(
            collective_id=0, has_side_effects=True, vmem_limit_bytes=60 * 2**20
        ),
        name="mla_backward",
    )(
        seg_map,
        hidden_in[0],
        proj_weight,
        proj_delta,
        norm_gain.reshape(1, LAT),
        jnp.asarray(freqs.astype(np.float32).reshape(1, HALF)),
        queries[0],
        out_grad[0],
    )
    return query_grad.reshape(1, NQ, H * KD), weight_grad


def solution(mesh):
    placed = (
        P("dp", "ctx", None),
        P("ctx", None),
        P("ctx", None),
        P(),
        P("dp", "ctx", None),
        P("dp", "ctx", None),
        P("dp", None),
    )
    return jax.shard_map(
        on_device,
        mesh=mesh,
        in_specs=placed,
        out_specs=(P("dp", "ctx", None), P("ctx", None)),
        check_vma=False,
    )
```

```python
import jax
import jax.numpy as jnp
import numpy as np
from jax import lax
from jax.experimental import pallas as pl
from jax.experimental.pallas import tpu as pltpu
from jax.sharding import PartitionSpec as P

H = 128
LAT = 512
ROPE = 64
KD = LAT + ROPE
HALF = ROPE // 2
NORM_EPS = 1e-06
SOFT_SCALE = 192.0 ** (-0.5)
ROPE_BASE = 10000.0

NX, NY, NZ = 4, 2, 8
ROWS = 128
NQ = 4
QR = NQ * H
DSH = 448
CHIP = 2 * DSH
D = 16 * DSH
LT = LAT // 128
WF = DSH * KD // 128
KF = ROWS * KD // 128
ZF = 64
W_ONE, W_A, W_B = 736, 544, 736
W_ODD = W_A + W_B
BF = jnp.bfloat16
F32 = jnp.float32
MESH = pl.DeviceIdType.MESH


def dot(a, b):
    return jnp.dot(a, b, preferred_element_type=F32)


def dot_t(a, b):
    return lax.dot_general(a, b, (((1,), (1,)), ((), ())), preferred_element_type=F32)


def t_dot(a, b):
    return lax.dot_general(a, b, (((0,), (0,)), ((), ())), preferred_element_type=F32)


def fold(part):
    n = part.shape[0] // 2
    return jnp.concatenate([part[:n], part[n:]], axis=1)


def unfold(part):
    return jnp.concatenate([part[:, :ROPE], part[:, ROPE:]], axis=0)


RING, KEYS, TWIN, ONCE = 0, 18, 36, 44
N_SEMS = ONCE + 50


class Net:
    def __init__(self, send_sems, recv_sems):
        self.send_sems, self.recv_sems = send_sems, recv_sems
        self.last, self.next = {}, {}

    def reuse(self, pool):
        self.next[pool] = 0

    def send(self, src, dst, to, pool=ONCE):
        i = pool + self.next.get(pool, 0)
        self.next[pool] = i + 1 - pool
        if i in self.last:
            self.last[i].wait_send()
        copy = pltpu.make_async_remote_copy(
            src_ref=src,
            dst_ref=dst,
            send_sem=self.send_sems.at[i],
            recv_sem=self.recv_sems.at[i],
            device_id=to,
            device_id_type=MESH,
        )
        copy.start()
        self.last[i] = copy
        return copy

    def sent(self, *copies):
        for i, copy in list(self.last.items()):
            if any(copy is c for c in copies):
                copy.wait_send()
                del self.last[i]

    def finish(self):
        for i in sorted(self.last):
            self.last[i].wait_send()


def kernel(
    seg_in, hid, w_ref, dw_ref, gain_ref, freq_ref, q_in, g_in,
    qg_out, agz,
    seg, q_raw, g_raw, q_ref, g_ref, own_hid, hidw, hidt, wbuf, acc, prec, unit_ref, inv_ref, trig,
    kflat, kbuf, e_ref, gp_ref, wt_ref, gs_ref, m_ref, l_ref, mj_ref, rd_ref,
    pf, pb, pr, qacc,
    b1s, b1r, a1s, a1r, a2s, a2r, a3s, a3r, b2s, b2r, b3s, b3r, t_b,
    gflat, gbuf, hrecv, h_t, term, tsend, trecv,
    arflat, arz, arl, far_half, near_half, qg_ref,
    send_sems, recv_sems, local_sems,
):
    c, d = lax.axis_index("ctx"), lax.axis_index("dp")
    x, y, core = lax.div(c, 4), lax.rem(lax.div(c, 2), 2), lax.rem(c, 2)
    yh, z = lax.div(d, NZ), lax.rem(d, NZ)
    xr, xl, xo, yo = lax.rem(x + 1, 4), lax.rem(x + 3, 4), lax.rem(x + 2, 4), 1 - y
    sib = 1 - core

    def at(xx, yy, cc=core):
        return {"ctx": xx * 4 + yy * 2 + cc}

    right, left, across, twin = at(xr, y), at(xl, y), at(x, yo), at(x, y, sib)

    def chip(xx, yy):
        return xx * 2 + yy

    others = [(xr, y), (xl, y), (x, yo), (xo, y), (xr, yo), (xl, yo), (xo, yo)]
    senders = [(xl, y), (xr, y), (x, yo), (xo, y), (xl, yo), (xr, yo), (xo, yo)]
    z_up = {"dp": yh * NZ + lax.rem(z + 1, NZ)}
    z_down = {"dp": yh * NZ + lax.rem(z + NZ - 1, NZ)}
    sequences = [
        lax.rem(yh + k // NZ, 2) * NZ + lax.rem(z + k % NZ, NZ) for k in range(1, 2 * NZ)
    ]

    barrier = pltpu.get_barrier_semaphore()
    peers = [right, left, across, twin] + [{"dp": dd} for dd in sequences]
    for peer in peers:
        pl.semaphore_signal(barrier, inc=1, device_id=peer, device_id_type=MESH)
    own_hidden = pltpu.make_async_copy(hid, own_hid, local_sems.at[0])
    own_hidden.start()
    own_queries = pltpu.make_async_copy(q_in, q_raw, local_sems.at[1])
    own_queries.start()
    own_grads = pltpu.make_async_copy(g_in, g_raw, local_sems.at[2])
    own_grads.start()
    own_segments = pltpu.make_async_copy(seg_in, seg, local_sems.at[3])
    own_segments.start()
    perturbed = (w_ref[...].astype(F32) + dw_ref[...].astype(F32)).astype(BF)
    mine = chip(x, y)
    for j in range(LT):
        wbuf[mine, pl.ds(DSH * j, DSH), :] = perturbed[:, 128 * j : 128 * j + 128]
    wbuf[mine, pl.ds(DSH * LT, DSH // 2), :] = fold(perturbed[:, LAT:])
    pl.semaphore_wait(barrier, len(peers))

    net = Net(send_sems, recv_sems)

    def all_gather(pool, buf, slot, base, n_a, n_b, idle, on_block):
        h_a, h_b = n_a // 2, n_b // 2

        def send(xx, yy, lo, n, to):
            ref = buf.at[slot(xx, yy), pl.ds(pl.multiple_of(base + lo, 16), n)]
            return net.send(ref, ref, to, pool)

        a_r = send(x, y, 0, n_a, right)
        a_l = send(x, y, 0, n_a, left)
        b_y = send(x, y, n_a, n_b, across)
        b_r = send(x, y, n_a, n_b, right)
        b_l = send(x, y, n_a, n_b, left)
        a_y = send(x, y, 0, n_a, across)
        idle[0]()
        on_block(x, y)
        b_y.wait_recv()
        bp_r = send(x, yo, n_a, n_b, right)
        bp_l = send(x, yo, n_a, n_b, left)
        a_r.wait_recv()
        a_r2 = send(xl, y, 0, h_a, right)
        a_yl = send(xl, y, 0, n_a, across)
        a_l.wait_recv()
        a_l2 = send(xr, y, h_a, h_a, left)
        a_yr = send(xr, y, 0, n_a, across)
        b_r.wait_recv()
        b_r2 = send(xl, y, n_a, h_b, right)
        b_l.wait_recv()
        b_l2 = send(xr, y, n_a + h_b, h_b, left)
        idle[1]()
        on_block(xl, y)
        on_block(xr, y)
        a_y.wait_recv()
        on_block(x, yo)
        bp_r.wait_recv()
        bp_r2 = send(xl, yo, n_a, h_b, right)
        bp_l.wait_recv()
        bp_l2 = send(xr, yo, n_a + h_b, h_b, left)
        a_r2.wait_recv()
        a_y1 = send(xo, y, 0, h_a, across)
        a_l2.wait_recv()
        a_y2 = send(xo, y, h_a, h_a, across)
        idle[2]()
        a_yl.wait_recv()
        on_block(xl, yo)
        a_yr.wait_recv()
        on_block(xr, yo)
        b_r2.wait_recv()
        b_l2.wait_recv()
        on_block(xo, y)
        bp_r2.wait_recv()
        bp_l2.wait_recv()
        a_y1.wait_recv()
        a_y2.wait_recv()
        on_block(xo, yo)

    def nothing():
        pass

    def angles():
        pos = (seg[0, c] * ROWS + lax.broadcasted_iota(jnp.int32, (ROWS, HALF), 0)).astype(F32)
        angle = pos * freq_ref[...]
        trig[:, :HALF] = jnp.cos(angle)
        trig[:, HALF:] = jnp.sin(angle)
        acc[...] = jnp.zeros_like(acc)

    def heads_to_rows(src, dst, width):
        def body(i, _):
            pieces = []
            for k in range(2):
                lo = pl.multiple_of((2 * i + k) * 2 * width, 128)
                block = src[:, pl.ds(lo, 2 * width)].astype(F32)
                pieces += [block[:, :width], block[:, width:]]
            rows = pl.ds(pl.multiple_of(i * 16, 16), 16)
            dst[rows, :] = jnp.concatenate(pieces, axis=0).astype(BF)
            return 0

        lax.fori_loop(0, QR // 16, body, 0)

    def hidden_windows():
        own_segments.wait()
        angles()
        own_hidden.wait()
        for i in range(NX * NY):
            pad = slice(512 * i + DSH, 512 * i + 512)
            hidw[:ROWS, pad] = jnp.zeros((ROWS, 512 - DSH), BF)
            hidt[:, pad] = jnp.zeros((ROWS, 512 - DSH), BF)

        for cc in range(2):

            @pl.when(core == cc)
            def _():
                for i in range(NX * NY):
                    lo, other = CHIP * i + DSH * cc, CHIP * i + DSH * (1 - cc)
                    hidw[:ROWS, 512 * i : 512 * i + DSH] = own_hid[:, lo : lo + DSH]
                    hidt[:, 512 * i : 512 * i + DSH] = own_hid[:, other : other + DSH]

        twin_hidden.append(net.send(hidt, hidw.at[pl.ds(ROWS, ROWS)], twin))
        hrecv[mine] = own_hid[:, pl.ds(pl.multiple_of(mine * CHIP, 128), CHIP)]

    twin_hidden = []

    def query_rows():
        own_queries.wait()
        heads_to_rows(q_raw, q_ref, KD)

    def grad_rows():
        own_grads.wait()
        heads_to_rows(g_raw, g_ref, LAT)

    def project(xx, yy):
        p = chip(xx, yy)
        lhs = hidw[:, pl.ds(pl.multiple_of(p * 512, 512), DSH)]
        tiles = [wbuf[p, pl.ds(DSH * j, DSH), :] for j in range(LT)]
        for j in range(0, LT, 2):
            acc[:, 128 * j : 128 * j + 256] += dot(
                lhs, jnp.concatenate([tiles[j], tiles[j + 1]], axis=1)
            )
        acc[:, LAT:] += dot(lhs, unfold(wbuf[p, pl.ds(DSH * LT, DSH // 2), :]))

    odd = lax.rem(z, 2)
    from_z = []
    parts = []

    def to_chip(k):
        xx, yy = others[k]
        columns = pl.ds(pl.multiple_of(chip(xx, yy) * CHIP, 128), CHIP)
        parts.append(net.send(own_hid.at[:, columns], hrecv.at[mine], at(xx, yy)))

    def project_next():
        xx, yy, copies = from_z.pop(0)
        for copy in copies:
            copy.wait_recv()
        project(xx, yy)

    def on_weights(xx, yy):
        def send(lo, n, to):
            ref = wbuf.at[chip(xx, yy), pl.ds(pl.multiple_of(odd * W_ODD + lo, 16), n)]
            return net.send(ref, ref, to)

        k = n_blocks[0]
        n_blocks[0] += 1
        if k == 0:
            copies = []
        elif k == 7:
            copies = [send(0, W_ONE // 2, z_up), send(W_ONE // 2, W_ONE // 2, z_down)]
        else:
            copies = [send(0, W_ONE, z_up if k in (1, 3, 4) else z_down)]
        from_z.append((xx, yy, copies))
        if k == 4:
            for i in (0, 1, 2):
                to_chip(i)
            twin_hidden[0].wait_recv()
        if k == 6:
            for i in (4, 5):
                to_chip(i)
        if k >= 4:
            project_next()
        if k == 7:
            while from_z:
                project_next()

    n_blocks = [0]
    idle = (hidden_windows, query_rows, grad_rows)
    all_gather(RING, wbuf, chip, odd * W_ONE, W_A, W_B, idle, on_weights)
    swap = net.send(acc.at[pl.ds(ROWS, ROWS)], prec, twin)
    swap.wait_recv()
    projected = acc[:ROWS, :] + prec[...]

    latent = projected[:, :LAT]
    inverse = lax.rsqrt(jnp.mean(latent * latent, axis=-1, keepdims=True) + NORM_EPS)
    unit = latent * inverse
    unit_ref[...] = unit
    inv_ref[...] = jnp.broadcast_to(inverse, (ROWS, 128))
    key_latent = (unit * gain_ref[...]).astype(BF)
    cosine, sine = trig[:, :HALF], trig[:, HALF:]
    first_half, second_half = projected[:, LAT : LAT + HALF], projected[:, LAT + HALF :]
    key_rope = jnp.concatenate(
        [first_half * cosine - second_half * sine, second_half * cosine + first_half * sine],
        axis=-1,
    )
    for j in range(LT):
        kflat[c, pl.ds(ROWS * j, ROWS), :] = key_latent[:, 128 * j : 128 * j + 128]
    kflat[c, pl.ds(ROWS * LT, ROWS // 2), :] = fold(key_rope).astype(BF)

    def slot(xx, yy):
        return xx * 4 + yy * 2 + core

    waiting = []

    def pair():
        copy, xx, yy = waiting.pop(0)
        copy.wait_recv()
        scores(xx, yy)

    def on_key(xx, yy):
        ref = kflat.at[slot(xx, yy)]
        waiting.append((net.send(ref, ref, twin, TWIN), xx, yy))
        if len(waiting) > 1:
            pair()

    def unpack(flat, rows, lo):
        for j in range(LT):
            rows[pl.ds(lo, ROWS), 128 * j : 128 * j + 128] = flat[pl.ds(ROWS * j, ROWS), :]
        rows[pl.ds(lo, ROWS), LAT:] = unfold(flat[pl.ds(ROWS * LT, ROWS // 2), :])

    def chip_rows(p):
        return pl.ds(pl.multiple_of(p * 256, 256), 256)

    query_pos = (
        seg[0, c] * ROWS
        + (lax.rem(lax.broadcasted_iota(jnp.int32, (1, QR), 1), NQ) + 1) * (ROWS // NQ)
        - 1
    )

    def start_scores():
        m_ref[...] = jnp.full_like(m_ref, -jnp.inf)
        l_ref[...] = jnp.zeros_like(l_ref)

    def scores(xx, yy):
        p = chip(xx, yy)
        for cc in range(2):
            unpack(kflat.at[2 * p + cc], kbuf, pl.multiple_of(p * 256 + 128 * cc, 128))
        rows = chip_rows(p)
        row = lax.broadcasted_iota(jnp.int32, (256, 1), 0)
        key_pos = (
            jnp.where(row < ROWS, seg[0, 2 * p], seg[0, 2 * p + 1]) * ROWS + lax.rem(row, ROWS)
        )
        s = SOFT_SCALE * dot_t(kbuf[rows, :], q_ref[...])
        s = jnp.where(key_pos <= query_pos, s, -jnp.inf)
        old = m_ref[...]
        new = jnp.maximum(old, jnp.max(s, axis=0, keepdims=True))
        e = jnp.exp(s - new)
        e_ref[rows, :] = e
        m_ref[...] = new
        mj_ref[p] = new
        l_ref[...] = l_ref[...] * jnp.exp(old - new) + jnp.sum(e, axis=0, keepdims=True)
        gp_ref[rows, :] = dot_t(kbuf[rows, :LAT], g_ref[...])

    all_gather(KEYS, kflat, slot, 0, 256, 320, (start_scores, nothing, nothing), on_key)

    to_chip(3)
    to_chip(6)
    pair()

    scale_by = 1.0 / l_ref[...]
    top = m_ref[...]
    rd_ref[...] = jnp.zeros_like(rd_ref)
    step = 64

    def weigh(i, _):
        rows = pl.ds(pl.multiple_of(i * step, step), step)
        factor = jnp.exp(mj_ref[lax.div(i, 256 // step)] - top) * scale_by
        weights = (e_ref[rows, :] * factor).astype(BF)
        wt_ref[rows, :] = weights
        rd_ref[...] += jnp.sum(weights.astype(F32) * gp_ref[rows, :], axis=0, keepdims=True)
        return 0

    lax.fori_loop(0, 2048 // step, weigh, 0)

    arrivals = [(x, y), (xl, y), (xr, y), (x, yo), (xl, yo), (xr, yo), (xo, y), (xo, yo)]

    def turn(i):
        if i > 0:
            parts[i - 1].wait_recv()
        h_t[:, 128 * i : 128 * i + 128] = hrecv[chip(*arrivals[i])].T

    def key_gradient(xx, yy, i):
        p = chip(xx, yy)
        rows = chip_rows(p)
        factor = jnp.exp(mj_ref[p] - m_ref[...]) * (SOFT_SCALE / l_ref[...])
        gs = (e_ref[rows, :] * factor * (gp_ref[rows, :] - rd_ref[...])).astype(BF)
        gs_ref[rows, :] = gs
        lat = dot(gs, q_ref[:, :LAT]) + dot(wt_ref[rows, :], g_ref[...])
        rope = dot(gs, q_ref[:, LAT:])
        for cc in range(2):
            half = slice(cc * ROWS, cc * ROWS + ROWS)
            for j in range(LT):
                tile = lat[half, 128 * j : 128 * j + 128]
                pf[i, cc, pl.ds(ROWS * j, ROWS), :] = tile
                pb[i, cc, pl.ds(ROWS * j, ROWS), :] = tile.astype(BF)
            tile = fold(rope[half])
            pf[i, cc, pl.ds(ROWS * LT, ROWS // 2), :] = tile
            pb[i, cc, pl.ds(ROWS * LT, ROWS // 2), :] = tile.astype(BF)
        return net.send(pb.at[i, sib], pr.at[i], twin)

    n_a, n_b = 256, 320
    h_a, h_b = n_a // 2, n_b // 2

    def summed(i, copy):
        copy.wait_recv()
        return pf[i, core] + pr[i].astype(F32)

    order = [(xo, yo), (xo, y), (xl, yo), (xr, yo), (x, yo), (xl, y), (xr, y), (x, y)]
    OO, OY, LO, RO, SO, LY, RY, SY = range(8)
    copies = [key_gradient(*order[0], 0), key_gradient(*order[1], 1)]
    net.reuse(RING)
    sums = {}
    a1 = []
    b1 = []
    for i in range(8):
        if i + 2 < 8:
            copies.append(key_gradient(*order[i + 2], i + 2))
        block = summed(i, copies[i])
        pf[i, core] = block
        if i in (OO, OY):
            yi = 1 if i == OO else 0
            a1s[yi, 0] = block[:h_a].astype(BF)
            a1s[yi, 1] = block[h_a:n_a].astype(BF)
            a1.append(net.send(a1s.at[yi, 0], a1r.at[yi, 0], right, RING))
            a1.append(net.send(a1s.at[yi, 1], a1r.at[yi, 1], left, RING))
        if i in (OO, LO, RO, SO):
            bi = {OO: 0, LO: 1, RO: 2, SO: 3}[i]
            b1s[bi] = block[n_a:].astype(BF)
            b1.append(net.send(b1s.at[bi], b1r.at[bi], across, RING))

    def own(i, lo, n):
        return pf[i, core, pl.ds(lo, n), :]

    def query_gradient():
        qacc[...] = jnp.zeros_like(qacc)

        def body(p, _):
            rows = chip_rows(p)
            qacc[...] += t_dot(gs_ref[rows, :], kbuf[rows, :])
            return 0

        lax.fori_loop(0, NX * NY, body, 0)

    def rows_to_heads():
        def body(i, _):
            rows = qacc[pl.ds(pl.multiple_of(i * 16, 16), 16), :]
            heads = jnp.concatenate([rows[4 * k : 4 * k + 4] for k in range(4)], axis=1)
            qg_ref[:, pl.ds(pl.multiple_of(i * 4 * KD, 128), 4 * KD)] = heads.astype(BF)
            return 0

        lax.fori_loop(0, QR // 16, body, 0)

    b1[0].wait_recv()
    t_b[0] = own(OY, n_a, n_b) + b1r[0].astype(F32)
    b2s[0] = t_b[0, :h_b].astype(BF)
    b2s[1] = t_b[0, h_b:].astype(BF)
    b2 = [net.send(b2s.at[0], b2r.at[0], right, RING), net.send(b2s.at[1], b2r.at[1], left, RING)]
    for copy in a1:
        copy.wait_recv()
    a2 = []
    for yi, (il, ir) in enumerate(((LY, RY), (LO, RO))):
        a2s[yi, 0, :h_a] = (own(ir, 0, h_a) + a1r[yi, 0].astype(F32)).astype(BF)
        a2s[yi, 0, h_a:] = own(ir, h_a, h_a).astype(BF)
        a2s[yi, 1, :h_a] = own(il, 0, h_a).astype(BF)
        a2s[yi, 1, h_a:] = (own(il, h_a, h_a) + a1r[yi, 1].astype(F32)).astype(BF)
        a2.append(net.send(a2s.at[yi, 0], a2r.at[yi, 0], right, RING))
        a2.append(net.send(a2s.at[yi, 1], a2r.at[yi, 1], left, RING))
    for i in range(6):
        turn(i)
    for copy in b1[1:]:
        copy.wait_recv()
    t_b[1] = own(LY, n_a, n_b) + b1r[1].astype(F32)
    t_b[2] = own(RY, n_a, n_b) + b1r[2].astype(F32)
    t_b[3] = own(SY, n_a, n_b) + b1r[3].astype(F32)
    for copy in b2:
        copy.wait_recv()
    b3s[0, :h_b] = (t_b[2, :h_b] + b2r[0].astype(F32)).astype(BF)
    b3s[0, h_b:] = t_b[2, h_b:].astype(BF)
    b3s[1, :h_b] = t_b[1, :h_b].astype(BF)
    b3s[1, h_b:] = (t_b[1, h_b:] + b2r[1].astype(F32)).astype(BF)
    b3 = [net.send(b3s.at[0], b3r.at[0], right, RING), net.send(b3s.at[1], b3r.at[1], left, RING)]
    for copy in a2:
        copy.wait_recv()
    a3s[...] = (own(SO, 0, n_a) + a2r[1, 0].astype(F32) + a2r[1, 1].astype(F32)).astype(BF)
    a3 = net.send(a3s, a3r, across, RING)
    for copy in b3:
        copy.wait_recv()
    grad_b = t_b[3] + b3r[0].astype(F32) + b3r[1].astype(F32)
    a3.wait_recv()
    grad_a = (
        own(SY, 0, n_a)
        + a2r[0, 0].astype(F32)
        + a2r[0, 1].astype(F32)
        + a3r[...].astype(F32)
    )

    grad_latent = jnp.concatenate(
        [grad_a[:ROWS], grad_a[ROWS:], grad_b[:ROWS], grad_b[ROWS : 2 * ROWS]], axis=1
    )
    grad_rope = unfold(grad_b[2 * ROWS :])
    unit = unit_ref[...]
    scaled = grad_latent * gain_ref[...]
    grad_latent = inv_ref[:, :1] * (
        scaled - unit * jnp.mean(scaled * unit, axis=-1, keepdims=True)
    )
    cosine, sine = trig[:, :HALF], trig[:, HALF:]
    upper, lower = grad_rope[:, :HALF], grad_rope[:, HALF:]
    grad_rope = jnp.concatenate(
        [upper * cosine + lower * sine, lower * cosine - upper * sine], axis=-1
    )
    for j in range(LT):
        gflat[c, pl.ds(ROWS * j, ROWS), :] = grad_latent[:, 128 * j : 128 * j + 128].astype(BF)
    gflat[c, pl.ds(ROWS * LT, ROWS // 2), :] = fold(grad_rope).astype(BF)

    blocks = []

    def add_term(xx, yy):
        k = len(blocks)
        blocks.append(k)
        if k >= 6:
            turn(k)
        unpack(gflat.at[slot(xx, yy)], gbuf, 128 * k)
        if k == 1:
            term[...] = dot(h_t[:, :256], gbuf[:256, :])
        elif k % 2:
            two = slice(128 * k - 128, 128 * k + 128)
            term[...] += dot(h_t[:, two], gbuf[two, :])

    net.reuse(KEYS)
    all_gather(KEYS, gflat, slot, 0, 256, 320, (nothing, nothing, nothing), add_term)

    def columns_of(first, lo, hi):
        rows = pl.ds(pl.multiple_of(first, 64), DSH)
        for j in range(lo, hi):
            yield pl.ds(DSH * j, DSH), term[rows, 128 * j : 128 * j + 128]
        if hi == LT:
            yield pl.ds(DSH * LT, DSH // 2), fold(term[rows, LAT:])

    swaps = []
    for lo, hi, first, last in ((0, 2, 0, 2 * DSH), (2, LT, 2 * DSH, WF)):
        for at_rows, part in columns_of(sib * DSH, lo, hi):
            tsend[at_rows, :] = part.astype(BF)
        flat = pl.ds(first, last - first)
        swaps.append(net.send(tsend.at[flat], trecv.at[flat], twin))

    for copy, lo, hi in zip(swaps, (0, 2), (2, LT), strict=True):
        copy.wait_recv()
        for at_rows, part in columns_of(core * DSH, lo, hi):
            arflat[at_rows, :] = (part + trecv[at_rows, :].astype(F32)).astype(BF)
    arflat[pl.ds(WF, 32 * ZF - WF), :] = jnp.zeros((32 * ZF - WF, 128), BF)

    def part_of(dd):
        return pl.ds(pl.multiple_of(dd * ZF, ZF), ZF)

    def half_of(yy, zz=0, n=NZ * ZF):
        return pl.ds(pl.multiple_of((2 + yy) * NZ * ZF + zz * ZF, ZF), n)

    opposite = {"dp": (1 - yh) * NZ + z}
    level = [lax.rem(z + k, NZ) for k in range(1, NZ)]
    first = net.send(arflat.at[half_of(1 - yh)], far_half, opposite)
    sums_in = [
        net.send(arflat.at[part_of(dd)], arz.at[k], {"dp": dd}) for k, dd in enumerate(sequences)
    ]
    first.wait_recv()
    near_half[...] = (arflat[half_of(yh), :].astype(F32) + far_half[...].astype(F32)).astype(BF)
    level_in = [
        net.send(near_half.at[part_of(zz)], arl.at[k], {"dp": yh * NZ + zz})
        for k, zz in enumerate(level)
    ]
    query_gradient()
    total = near_half[part_of(z), :].astype(F32)
    for k, copy in enumerate(level_in):
        copy.wait_recv()
        total += arl[k].astype(F32)
    net.reuse(KEYS)
    own_rows = half_of(yh, z, ZF)
    agz[own_rows, :] = total.astype(BF)
    level_out = [
        net.send(agz.at[own_rows], agz.at[own_rows], {"dp": yh * NZ + zz}, KEYS) for zz in level
    ]
    total = arflat[part_of(d), :].astype(F32)
    for k, copy in enumerate(sums_in):
        copy.wait_recv()
        total += arz[k].astype(F32)
    agz[part_of(d), :] = total.astype(BF)
    net.reuse(RING)
    sums_out = [
        net.send(agz.at[part_of(d)], agz.at[part_of(d)], {"dp": dd}, RING) for dd in sequences
    ]
    for copy in level_out:
        copy.wait_recv()
    sums_out.append(net.send(agz.at[half_of(yh)], agz.at[half_of(yh)], opposite, KEYS))
    rows_to_heads()
    done = pltpu.make_async_copy(qg_ref, qg_out, local_sems.at[4])
    done.start()
    for copy in sums_out:
        copy.wait_recv()
    done.wait()
    net.finish()
    assert ONCE + net.next[ONCE] == N_SEMS


def hand_over(qg_in, flat, qg_out, wg_ref):
    for j in range(LT):
        wg_ref[:, 128 * j : 128 * j + 128] = flat[pl.ds(DSH * j, DSH), :].astype(F32)
    wg_ref[:, LAT:] = unfold(flat[pl.ds(DSH * LT, DSH // 2), :].astype(F32))
    qg_out[...] = qg_in[...]


def on_device(hidden_in, proj_weight, proj_delta, norm_gain, queries, out_grad, seg_map):
    vmem = pl.BlockSpec(memory_space=pltpu.VMEM)
    freqs = np.float32(ROPE_BASE) ** (-(np.arange(HALF, dtype=np.float32) * 2 / ROPE))
    v = pltpu.VMEM
    scratch = [
        pltpu.SMEM((1, 16), jnp.int32),
        v((NQ, H * KD), BF), v((NQ, H * LAT), BF), v((QR, KD), BF), v((QR, LAT), BF),
        v((ROWS, D), BF), v((2 * ROWS, 8 * 512), BF), v((ROWS, 8 * 512), BF), v((8, WF, 128), BF),
        v((2 * ROWS, KD), F32), v((ROWS, KD), F32), v((ROWS, LAT), F32), v((ROWS, 128), F32),
        v((ROWS, ROPE), F32),
        v((16, KF, 128), BF), v((2048, KD), BF), v((2048, QR), F32), v((2048, QR), F32),
        v((2048, QR), BF), v((2048, QR), BF), v((1, QR), F32), v((1, QR), F32),
        v((8, 1, QR), F32), v((1, QR), F32),
        v((8, 2, KF, 128), F32), v((8, 2, KF, 128), BF), v((8, KF, 128), BF), v((QR, KD), F32),
        v((4, 320, 128), BF), v((4, 320, 128), BF),
        v((2, 2, 128, 128), BF), v((2, 2, 128, 128), BF),
        v((2, 2, 256, 128), BF), v((2, 2, 256, 128), BF),
        v((256, 128), BF), v((256, 128), BF),
        v((2, 160, 128), BF), v((2, 160, 128), BF),
        v((2, 320, 128), BF), v((2, 320, 128), BF),
        v((4, 320, 128), F32),
        v((16, KF, 128), BF), v((1024, KD), BF),
        v((8, ROWS, CHIP), BF), v((CHIP, 1024), BF), v((CHIP, KD), F32),
        v((WF, 128), BF), v((WF, 128), BF),
        v((32 * ZF, 128), BF), v((15, ZF, 128), BF), v((7, ZF, 128), BF), v((8 * ZF, 128), BF),
        v((8 * ZF, 128), BF), v((NQ, H * KD), BF),
        pltpu.SemaphoreType.DMA((N_SEMS,)), pltpu.SemaphoreType.DMA((N_SEMS,)),
        pltpu.SemaphoreType.DMA((5,)),
    ]
    query_grad, flat = pl.pallas_call(
        kernel,
        out_shape=(
            jax.ShapeDtypeStruct((NQ, H * KD), BF),
            jax.ShapeDtypeStruct((32 * ZF, 128), BF),
        ),
        in_specs=[
            pl.BlockSpec(memory_space=pl.ANY),
            pl.BlockSpec(memory_space=pl.ANY),
        ]
        + [vmem] * 4
        + [pl.BlockSpec(memory_space=pl.ANY)] * 2,
        out_specs=(pl.BlockSpec(memory_space=pl.ANY), vmem),
        scratch_shapes=scratch,
        compiler_params=pltpu.CompilerParams(
            collective_id=0, has_side_effects=True, vmem_limit_bytes=60 * 2**20
        ),
        name="mla_backward",
    )(
        seg_map,
        hidden_in[0],
        proj_weight,
        proj_delta,
        norm_gain.reshape(1, LAT),
        jnp.asarray(freqs.astype(np.float32).reshape(1, HALF)),
        queries[0],
        out_grad[0],
    )
    query_grad, weight_grad = pl.pallas_call(
        hand_over,
        out_shape=(
            jax.ShapeDtypeStruct((NQ, H * KD), BF),
            jax.ShapeDtypeStruct((DSH, KD), F32),
        ),
        in_specs=[vmem, vmem],
        out_specs=(vmem, vmem),
        name="hand_over",
    )(query_grad, flat)
    return query_grad.reshape(1, NQ, H * KD), weight_grad


def solution(mesh):
    placed = (
        P("dp", "ctx", None),
        P("ctx", None),
        P("ctx", None),
        P(),
        P("dp", "ctx", None),
        P("dp", "ctx", None),
        P("dp", None),
    )
    return jax.shard_map(
        on_device,
        mesh=mesh,
        in_specs=placed,
        out_specs=(P("dp", "ctx", None), P("ctx", None)),
        check_vma=False,
    )
```

```python
import jax
import jax.numpy as jnp
import numpy as np
from jax import lax
from jax.experimental import pallas as pl
from jax.experimental.pallas import tpu as pltpu
from jax.sharding import PartitionSpec as P

H = 128
LAT = 512
ROPE = 64
KD = LAT + ROPE
HALF = ROPE // 2
NORM_EPS = 1e-06
SOFT_SCALE = 192.0 ** (-0.5)
ROPE_BASE = 10000.0

NX, NY, NZ = 4, 2, 8
ROWS = 128
NQ = 4
QR = NQ * H
DSH = 448
CHIP = 2 * DSH
D = 16 * DSH
LT = LAT // 128
WF = DSH * KD // 128
KF = ROWS * KD // 128
ZF = 64
W_ONE, W_A, W_B = 736, 544, 736
W_ODD = W_A + W_B
BF = jnp.bfloat16
F32 = jnp.float32
MESH = pl.DeviceIdType.MESH


def dot(a, b):
    return jnp.dot(a, b, preferred_element_type=F32)


def dot_t(a, b):
    return lax.dot_general(a, b, (((1,), (1,)), ((), ())), preferred_element_type=F32)


def t_dot(a, b):
    return lax.dot_general(a, b, (((0,), (0,)), ((), ())), preferred_element_type=F32)


def fold(part):
    n = part.shape[0] // 2
    return jnp.concatenate([part[:n], part[n:]], axis=1)


def unfold(part):
    return jnp.concatenate([part[:, :ROPE], part[:, ROPE:]], axis=0)


RING, KEYS, TWIN, ONCE = 0, 18, 36, 44
N_SEMS = ONCE + 50


class Net:
    def __init__(self, send_sems, recv_sems):
        self.send_sems, self.recv_sems = send_sems, recv_sems
        self.last, self.next = {}, {}

    def reuse(self, pool):
        self.next[pool] = 0

    def send(self, src, dst, to, pool=ONCE):
        i = pool + self.next.get(pool, 0)
        self.next[pool] = i + 1 - pool
        if i in self.last:
            self.last[i].wait_send()
        copy = pltpu.make_async_remote_copy(
            src_ref=src,
            dst_ref=dst,
            send_sem=self.send_sems.at[i],
            recv_sem=self.recv_sems.at[i],
            device_id=to,
            device_id_type=MESH,
        )
        copy.start()
        self.last[i] = copy
        return copy

    def sent(self, *copies):
        for i, copy in list(self.last.items()):
            if any(copy is c for c in copies):
                copy.wait_send()
                del self.last[i]

    def finish(self):
        for i in sorted(self.last):
            self.last[i].wait_send()


def kernel(
    seg_in, hid, w_in, dw_in, gain_in, freq_in, q_in, g_in,
    qg_out, agz,
    seg, w_ref, dw_ref, gain_ref, freq_ref, q_raw, g_raw, q_ref, g_ref, own_hid, hidw, hidt, wbuf, acc, prec, unit_ref, inv_ref, trig,
    kflat, kbuf, e_ref, gp_ref, wt_ref, gs_ref, m_ref, l_ref, mj_ref, rd_ref,
    pf, pb, pr, qacc,
    b1s, b1r, a1s, a1r, a2s, a2r, a3s, a3r, b2s, b2r, b3s, b3r, t_b,
    gflat, gbuf, hrecv, h_t, term, tsend, trecv,
    arflat, arz, arl, far_half, near_half, qg_ref,
    send_sems, recv_sems, local_sems,
):
    c, d = lax.axis_index("ctx"), lax.axis_index("dp")
    x, y, core = lax.div(c, 4), lax.rem(lax.div(c, 2), 2), lax.rem(c, 2)
    yh, z = lax.div(d, NZ), lax.rem(d, NZ)
    xr, xl, xo, yo = lax.rem(x + 1, 4), lax.rem(x + 3, 4), lax.rem(x + 2, 4), 1 - y
    sib = 1 - core

    def at(xx, yy, cc=core):
        return {"ctx": xx * 4 + yy * 2 + cc}

    right, left, across, twin = at(xr, y), at(xl, y), at(x, yo), at(x, y, sib)

    def chip(xx, yy):
        return xx * 2 + yy

    others = [(xr, y), (xl, y), (x, yo), (xo, y), (xr, yo), (xl, yo), (xo, yo)]
    senders = [(xl, y), (xr, y), (x, yo), (xo, y), (xl, yo), (xr, yo), (xo, yo)]
    z_up = {"dp": yh * NZ + lax.rem(z + 1, NZ)}
    z_down = {"dp": yh * NZ + lax.rem(z + NZ - 1, NZ)}
    sequences = [
        lax.rem(yh + k // NZ, 2) * NZ + lax.rem(z + k % NZ, NZ) for k in range(1, 2 * NZ)
    ]

    barrier = pltpu.get_barrier_semaphore()
    peers = [right, left, across, twin] + [{"dp": dd} for dd in sequences]
    for peer in peers:
        pl.semaphore_signal(barrier, inc=1, device_id=peer, device_id_type=MESH)
    own_weights, own_deltas, own_hidden, own_segments, own_gain, own_freqs, own_queries, own_grads = [
        pltpu.make_async_copy(src, dst, local_sems.at[i])
        for i, (src, dst) in enumerate(
            (
                (w_in, w_ref),
                (dw_in, dw_ref),
                (hid, own_hid),
                (seg_in, seg),
                (gain_in, gain_ref),
                (freq_in, freq_ref),
                (q_in, q_raw),
                (g_in, g_raw),
            )
        )
    ]
    own_weights.start()
    own_deltas.start()
    own_hidden.start()
    own_segments.start()
    own_gain.start()
    own_freqs.start()
    own_queries.start()
    own_grads.start()
    own_weights.wait()
    own_deltas.wait()
    perturbed = (w_ref[...].astype(F32) + dw_ref[...].astype(F32)).astype(BF)
    mine = chip(x, y)
    for j in range(LT):
        wbuf[mine, pl.ds(DSH * j, DSH), :] = perturbed[:, 128 * j : 128 * j + 128]
    wbuf[mine, pl.ds(DSH * LT, DSH // 2), :] = fold(perturbed[:, LAT:])
    pl.semaphore_wait(barrier, len(peers))

    net = Net(send_sems, recv_sems)

    def all_gather(pool, buf, slot, base, n_a, n_b, idle, on_block):
        h_a, h_b = n_a // 2, n_b // 2

        def send(xx, yy, lo, n, to):
            ref = buf.at[slot(xx, yy), pl.ds(pl.multiple_of(base + lo, 16), n)]
            return net.send(ref, ref, to, pool)

        a_r = send(x, y, 0, n_a, right)
        a_l = send(x, y, 0, n_a, left)
        b_y = send(x, y, n_a, n_b, across)
        b_r = send(x, y, n_a, n_b, right)
        b_l = send(x, y, n_a, n_b, left)
        a_y = send(x, y, 0, n_a, across)
        idle[0]()
        on_block(x, y)
        b_y.wait_recv()
        bp_r = send(x, yo, n_a, n_b, right)
        bp_l = send(x, yo, n_a, n_b, left)
        a_r.wait_recv()
        a_r2 = send(xl, y, 0, h_a, right)
        a_yl = send(xl, y, 0, n_a, across)
        a_l.wait_recv()
        a_l2 = send(xr, y, h_a, h_a, left)
        a_yr = send(xr, y, 0, n_a, across)
        b_r.wait_recv()
        b_r2 = send(xl, y, n_a, h_b, right)
        b_l.wait_recv()
        b_l2 = send(xr, y, n_a + h_b, h_b, left)
        idle[1]()
        on_block(xl, y)
        on_block(xr, y)
        a_y.wait_recv()
        on_block(x, yo)
        bp_r.wait_recv()
        bp_r2 = send(xl, yo, n_a, h_b, right)
        bp_l.wait_recv()
        bp_l2 = send(xr, yo, n_a + h_b, h_b, left)
        a_r2.wait_recv()
        a_y1 = send(xo, y, 0, h_a, across)
        a_l2.wait_recv()
        a_y2 = send(xo, y, h_a, h_a, across)
        idle[2]()
        a_yl.wait_recv()
        on_block(xl, yo)
        a_yr.wait_recv()
        on_block(xr, yo)
        b_r2.wait_recv()
        b_l2.wait_recv()
        on_block(xo, y)
        bp_r2.wait_recv()
        bp_l2.wait_recv()
        a_y1.wait_recv()
        a_y2.wait_recv()
        on_block(xo, yo)

    def nothing():
        pass

    def angles():
        pos = (seg[0, c] * ROWS + lax.broadcasted_iota(jnp.int32, (ROWS, HALF), 0)).astype(F32)
        angle = pos * freq_ref[...]
        trig[:, :HALF] = jnp.cos(angle)
        trig[:, HALF:] = jnp.sin(angle)
        acc[...] = jnp.zeros_like(acc)

    def heads_to_rows(src, dst, width):
        def body(i, _):
            pieces = []
            for k in range(2):
                lo = pl.multiple_of((2 * i + k) * 2 * width, 128)
                block = src[:, pl.ds(lo, 2 * width)].astype(F32)
                pieces += [block[:, :width], block[:, width:]]
            rows = pl.ds(pl.multiple_of(i * 16, 16), 16)
            dst[rows, :] = jnp.concatenate(pieces, axis=0).astype(BF)
            return 0

        lax.fori_loop(0, QR // 16, body, 0)

    def hidden_windows():
        own_segments.wait()
        own_gain.wait()
        own_freqs.wait()
        angles()
        own_hidden.wait()
        for i in range(NX * NY):
            pad = slice(512 * i + DSH, 512 * i + 512)
            hidw[:ROWS, pad] = jnp.zeros((ROWS, 512 - DSH), BF)
            hidt[:, pad] = jnp.zeros((ROWS, 512 - DSH), BF)

        for cc in range(2):

            @pl.when(core == cc)
            def _():
                for i in range(NX * NY):
                    lo, other = CHIP * i + DSH * cc, CHIP * i + DSH * (1 - cc)
                    hidw[:ROWS, 512 * i : 512 * i + DSH] = own_hid[:, lo : lo + DSH]
                    hidt[:, 512 * i : 512 * i + DSH] = own_hid[:, other : other + DSH]

        twin_hidden.append(net.send(hidt, hidw.at[pl.ds(ROWS, ROWS)], twin))
        hrecv[mine] = own_hid[:, pl.ds(pl.multiple_of(mine * CHIP, 128), CHIP)]

    twin_hidden = []

    def query_rows():
        own_queries.wait()
        heads_to_rows(q_raw, q_ref, KD)

    def grad_rows():
        own_grads.wait()
        heads_to_rows(g_raw, g_ref, LAT)

    def project(xx, yy):
        p = chip(xx, yy)
        lhs = hidw[:, pl.ds(pl.multiple_of(p * 512, 512), DSH)]
        tiles = [wbuf[p, pl.ds(DSH * j, DSH), :] for j in range(LT)]
        for j in range(0, LT, 2):
            acc[:, 128 * j : 128 * j + 256] += dot(
                lhs, jnp.concatenate([tiles[j], tiles[j + 1]], axis=1)
            )
        acc[:, LAT:] += dot(lhs, unfold(wbuf[p, pl.ds(DSH * LT, DSH // 2), :]))

    odd = lax.rem(z, 2)
    from_z = []
    parts = []

    def to_chip(k):
        xx, yy = others[k]
        columns = pl.ds(pl.multiple_of(chip(xx, yy) * CHIP, 128), CHIP)
        parts.append(net.send(own_hid.at[:, columns], hrecv.at[mine], at(xx, yy)))

    def project_next():
        xx, yy, copies = from_z.pop(0)
        for copy in copies:
            copy.wait_recv()
        project(xx, yy)

    def on_weights(xx, yy):
        def send(lo, n, to):
            ref = wbuf.at[chip(xx, yy), pl.ds(pl.multiple_of(odd * W_ODD + lo, 16), n)]
            return net.send(ref, ref, to)

        k = n_blocks[0]
        n_blocks[0] += 1
        if k == 0:
            copies = []
        elif k == 7:
            copies = [send(0, W_ONE // 2, z_up), send(W_ONE // 2, W_ONE // 2, z_down)]
        else:
            copies = [send(0, W_ONE, z_up if k in (1, 3, 4) else z_down)]
        from_z.append((xx, yy, copies))
        if k == 4:
            for i in (0, 1, 2):
                to_chip(i)
            twin_hidden[0].wait_recv()
        if k == 6:
            for i in (4, 5):
                to_chip(i)
        if k >= 4:
            project_next()
        if k == 7:
            while from_z:
                project_next()

    n_blocks = [0]
    idle = (hidden_windows, query_rows, grad_rows)
    all_gather(RING, wbuf, chip, odd * W_ONE, W_A, W_B, idle, on_weights)
    swap = net.send(acc.at[pl.ds(ROWS, ROWS)], prec, twin)
    swap.wait_recv()
    projected = acc[:ROWS, :] + prec[...]

    latent = projected[:, :LAT]
    inverse = lax.rsqrt(jnp.mean(latent * latent, axis=-1, keepdims=True) + NORM_EPS)
    unit = latent * inverse
    unit_ref[...] = unit
    inv_ref[...] = jnp.broadcast_to(inverse, (ROWS, 128))
    key_latent = (unit * gain_ref[...]).astype(BF)
    cosine, sine = trig[:, :HALF], trig[:, HALF:]
    first_half, second_half = projected[:, LAT : LAT + HALF], projected[:, LAT + HALF :]
    key_rope = jnp.concatenate(
        [first_half * cosine - second_half * sine, second_half * cosine + first_half * sine],
        axis=-1,
    )
    for j in range(LT):
        kflat[c, pl.ds(ROWS * j, ROWS), :] = key_latent[:, 128 * j : 128 * j + 128]
    kflat[c, pl.ds(ROWS * LT, ROWS // 2), :] = fold(key_rope).astype(BF)

    def slot(xx, yy):
        return xx * 4 + yy * 2 + core

    waiting = []

    def pair():
        copy, xx, yy = waiting.pop(0)
        copy.wait_recv()
        scores(xx, yy)

    def on_key(xx, yy):
        ref = kflat.at[slot(xx, yy)]
        waiting.append((net.send(ref, ref, twin, TWIN), xx, yy))
        if len(waiting) > 1:
            pair()

    def unpack(flat, rows, lo):
        for j in range(LT):
            rows[pl.ds(lo, ROWS), 128 * j : 128 * j + 128] = flat[pl.ds(ROWS * j, ROWS), :]
        rows[pl.ds(lo, ROWS), LAT:] = unfold(flat[pl.ds(ROWS * LT, ROWS // 2), :])

    def chip_rows(p):
        return pl.ds(pl.multiple_of(p * 256, 256), 256)

    query_pos = (
        seg[0, c] * ROWS
        + (lax.rem(lax.broadcasted_iota(jnp.int32, (1, QR), 1), NQ) + 1) * (ROWS // NQ)
        - 1
    )

    def start_scores():
        m_ref[...] = jnp.full_like(m_ref, -jnp.inf)
        l_ref[...] = jnp.zeros_like(l_ref)

    def scores(xx, yy):
        p = chip(xx, yy)
        for cc in range(2):
            unpack(kflat.at[2 * p + cc], kbuf, pl.multiple_of(p * 256 + 128 * cc, 128))
        rows = chip_rows(p)
        row = lax.broadcasted_iota(jnp.int32, (256, 1), 0)
        key_pos = (
            jnp.where(row < ROWS, seg[0, 2 * p], seg[0, 2 * p + 1]) * ROWS + lax.rem(row, ROWS)
        )
        s = SOFT_SCALE * dot_t(kbuf[rows, :], q_ref[...])
        s = jnp.where(key_pos <= query_pos, s, -jnp.inf)
        old = m_ref[...]
        new = jnp.maximum(old, jnp.max(s, axis=0, keepdims=True))
        e = jnp.exp(s - new)
        e_ref[rows, :] = e
        m_ref[...] = new
        mj_ref[p] = new
        l_ref[...] = l_ref[...] * jnp.exp(old - new) + jnp.sum(e, axis=0, keepdims=True)
        gp_ref[rows, :] = dot_t(kbuf[rows, :LAT], g_ref[...])

    all_gather(KEYS, kflat, slot, 0, 256, 320, (start_scores, nothing, nothing), on_key)

    to_chip(3)
    to_chip(6)
    pair()

    scale_by = 1.0 / l_ref[...]
    top = m_ref[...]
    rd_ref[...] = jnp.zeros_like(rd_ref)
    step = 64

    def weigh(i, _):
        rows = pl.ds(pl.multiple_of(i * step, step), step)
        factor = jnp.exp(mj_ref[lax.div(i, 256 // step)] - top) * scale_by
        weights = (e_ref[rows, :] * factor).astype(BF)
        wt_ref[rows, :] = weights
        rd_ref[...] += jnp.sum(weights.astype(F32) * gp_ref[rows, :], axis=0, keepdims=True)
        return 0

    lax.fori_loop(0, 2048 // step, weigh, 0)

    arrivals = [(x, y), (xl, y), (xr, y), (x, yo), (xl, yo), (xr, yo), (xo, y), (xo, yo)]

    def turn(i):
        if i > 0:
            parts[i - 1].wait_recv()
        h_t[:, 128 * i : 128 * i + 128] = hrecv[chip(*arrivals[i])].T

    def key_gradient(xx, yy, i):
        p = chip(xx, yy)
        rows = chip_rows(p)
        factor = jnp.exp(mj_ref[p] - m_ref[...]) * (SOFT_SCALE / l_ref[...])
        gs = (e_ref[rows, :] * factor * (gp_ref[rows, :] - rd_ref[...])).astype(BF)
        gs_ref[rows, :] = gs
        lat = dot(gs, q_ref[:, :LAT]) + dot(wt_ref[rows, :], g_ref[...])
        rope = dot(gs, q_ref[:, LAT:])
        for cc in range(2):
            half = slice(cc * ROWS, cc * ROWS + ROWS)
            for j in range(LT):
                tile = lat[half, 128 * j : 128 * j + 128]
                pf[i, cc, pl.ds(ROWS * j, ROWS), :] = tile
                pb[i, cc, pl.ds(ROWS * j, ROWS), :] = tile.astype(BF)
            tile = fold(rope[half])
            pf[i, cc, pl.ds(ROWS * LT, ROWS // 2), :] = tile
            pb[i, cc, pl.ds(ROWS * LT, ROWS // 2), :] = tile.astype(BF)
        return net.send(pb.at[i, sib], pr.at[i], twin)

    n_a, n_b = 256, 320
    h_a, h_b = n_a // 2, n_b // 2

    def summed(i, copy):
        copy.wait_recv()
        return pf[i, core] + pr[i].astype(F32)

    order = [(xo, yo), (xo, y), (xl, yo), (xr, yo), (x, yo), (xl, y), (xr, y), (x, y)]
    OO, OY, LO, RO, SO, LY, RY, SY = range(8)
    copies = [key_gradient(*order[0], 0), key_gradient(*order[1], 1)]
    net.reuse(RING)
    sums = {}
    a1 = []
    b1 = []
    for i in range(8):
        if i + 2 < 8:
            copies.append(key_gradient(*order[i + 2], i + 2))
        block = summed(i, copies[i])
        pf[i, core] = block
        if i in (OO, OY):
            yi = 1 if i == OO else 0
            a1s[yi, 0] = block[:h_a].astype(BF)
            a1s[yi, 1] = block[h_a:n_a].astype(BF)
            a1.append(net.send(a1s.at[yi, 0], a1r.at[yi, 0], right, RING))
            a1.append(net.send(a1s.at[yi, 1], a1r.at[yi, 1], left, RING))
        if i in (OO, LO, RO, SO):
            bi = {OO: 0, LO: 1, RO: 2, SO: 3}[i]
            b1s[bi] = block[n_a:].astype(BF)
            b1.append(net.send(b1s.at[bi], b1r.at[bi], across, RING))

    def own(i, lo, n):
        return pf[i, core, pl.ds(lo, n), :]

    def query_gradient():
        qacc[...] = jnp.zeros_like(qacc)

        def body(p, _):
            rows = chip_rows(p)
            qacc[...] += t_dot(gs_ref[rows, :], kbuf[rows, :])
            return 0

        lax.fori_loop(0, NX * NY, body, 0)

    def rows_to_heads():
        def body(i, _):
            rows = qacc[pl.ds(pl.multiple_of(i * 16, 16), 16), :]
            heads = jnp.concatenate([rows[4 * k : 4 * k + 4] for k in range(4)], axis=1)
            qg_ref[:, pl.ds(pl.multiple_of(i * 4 * KD, 128), 4 * KD)] = heads.astype(BF)
            return 0

        lax.fori_loop(0, QR // 16, body, 0)

    b1[0].wait_recv()
    t_b[0] = own(OY, n_a, n_b) + b1r[0].astype(F32)
    b2s[0] = t_b[0, :h_b].astype(BF)
    b2s[1] = t_b[0, h_b:].astype(BF)
    b2 = [net.send(b2s.at[0], b2r.at[0], right, RING), net.send(b2s.at[1], b2r.at[1], left, RING)]
    for copy in a1:
        copy.wait_recv()
    a2 = []
    for yi, (il, ir) in enumerate(((LY, RY), (LO, RO))):
        a2s[yi, 0, :h_a] = (own(ir, 0, h_a) + a1r[yi, 0].astype(F32)).astype(BF)
        a2s[yi, 0, h_a:] = own(ir, h_a, h_a).astype(BF)
        a2s[yi, 1, :h_a] = own(il, 0, h_a).astype(BF)
        a2s[yi, 1, h_a:] = (own(il, h_a, h_a) + a1r[yi, 1].astype(F32)).astype(BF)
        a2.append(net.send(a2s.at[yi, 0], a2r.at[yi, 0], right, RING))
        a2.append(net.send(a2s.at[yi, 1], a2r.at[yi, 1], left, RING))
    for i in range(6):
        turn(i)
    for copy in b1[1:]:
        copy.wait_recv()
    t_b[1] = own(LY, n_a, n_b) + b1r[1].astype(F32)
    t_b[2] = own(RY, n_a, n_b) + b1r[2].astype(F32)
    t_b[3] = own(SY, n_a, n_b) + b1r[3].astype(F32)
    for copy in b2:
        copy.wait_recv()
    b3s[0, :h_b] = (t_b[2, :h_b] + b2r[0].astype(F32)).astype(BF)
    b3s[0, h_b:] = t_b[2, h_b:].astype(BF)
    b3s[1, :h_b] = t_b[1, :h_b].astype(BF)
    b3s[1, h_b:] = (t_b[1, h_b:] + b2r[1].astype(F32)).astype(BF)
    b3 = [net.send(b3s.at[0], b3r.at[0], right, RING), net.send(b3s.at[1], b3r.at[1], left, RING)]
    for copy in a2:
        copy.wait_recv()
    a3s[...] = (own(SO, 0, n_a) + a2r[1, 0].astype(F32) + a2r[1, 1].astype(F32)).astype(BF)
    a3 = net.send(a3s, a3r, across, RING)
    for copy in b3:
        copy.wait_recv()
    grad_b = t_b[3] + b3r[0].astype(F32) + b3r[1].astype(F32)
    a3.wait_recv()
    grad_a = (
        own(SY, 0, n_a)
        + a2r[0, 0].astype(F32)
        + a2r[0, 1].astype(F32)
        + a3r[...].astype(F32)
    )

    grad_latent = jnp.concatenate(
        [grad_a[:ROWS], grad_a[ROWS:], grad_b[:ROWS], grad_b[ROWS : 2 * ROWS]], axis=1
    )
    grad_rope = unfold(grad_b[2 * ROWS :])
    unit = unit_ref[...]
    scaled = grad_latent * gain_ref[...]
    grad_latent = inv_ref[:, :1] * (
        scaled - unit * jnp.mean(scaled * unit, axis=-1, keepdims=True)
    )
    cosine, sine = trig[:, :HALF], trig[:, HALF:]
    upper, lower = grad_rope[:, :HALF], grad_rope[:, HALF:]
    grad_rope = jnp.concatenate(
        [upper * cosine + lower * sine, lower * cosine - upper * sine], axis=-1
    )
    for j in range(LT):
        gflat[c, pl.ds(ROWS * j, ROWS), :] = grad_latent[:, 128 * j : 128 * j + 128].astype(BF)
    gflat[c, pl.ds(ROWS * LT, ROWS // 2), :] = fold(grad_rope).astype(BF)

    blocks = []

    def add_term(xx, yy):
        k = len(blocks)
        blocks.append(k)
        if k >= 6:
            turn(k)
        unpack(gflat.at[slot(xx, yy)], gbuf, 128 * k)
        if k == 1:
            term[...] = dot(h_t[:, :256], gbuf[:256, :])
        elif k % 2:
            two = slice(128 * k - 128, 128 * k + 128)
            term[...] += dot(h_t[:, two], gbuf[two, :])

    net.reuse(KEYS)
    all_gather(KEYS, gflat, slot, 0, 256, 320, (nothing, nothing, nothing), add_term)

    def columns_of(first, lo, hi):
        rows = pl.ds(pl.multiple_of(first, 64), DSH)
        for j in range(lo, hi):
            yield pl.ds(DSH * j, DSH), term[rows, 128 * j : 128 * j + 128]
        if hi == LT:
            yield pl.ds(DSH * LT, DSH // 2), fold(term[rows, LAT:])

    swaps = []
    for lo, hi, first, last in ((0, 2, 0, 2 * DSH), (2, LT, 2 * DSH, WF)):
        for at_rows, part in columns_of(sib * DSH, lo, hi):
            tsend[at_rows, :] = part.astype(BF)
        flat = pl.ds(first, last - first)
        swaps.append(net.send(tsend.at[flat], trecv.at[flat], twin))

    for copy, lo, hi in zip(swaps, (0, 2), (2, LT), strict=True):
        copy.wait_recv()
        for at_rows, part in columns_of(core * DSH, lo, hi):
            arflat[at_rows, :] = (part + trecv[at_rows, :].astype(F32)).astype(BF)
    arflat[pl.ds(WF, 32 * ZF - WF), :] = jnp.zeros((32 * ZF - WF, 128), BF)

    def part_of(dd):
        return pl.ds(pl.multiple_of(dd * ZF, ZF), ZF)

    def half_of(yy, zz=0, n=NZ * ZF):
        return pl.ds(pl.multiple_of((2 + yy) * NZ * ZF + zz * ZF, ZF), n)

    opposite = {"dp": (1 - yh) * NZ + z}
    level = [lax.rem(z + k, NZ) for k in range(1, NZ)]
    first = net.send(arflat.at[half_of(1 - yh)], far_half, opposite)
    sums_in = [
        net.send(arflat.at[part_of(dd)], arz.at[k], {"dp": dd}) for k, dd in enumerate(sequences)
    ]
    first.wait_recv()
    near_half[...] = (arflat[half_of(yh), :].astype(F32) + far_half[...].astype(F32)).astype(BF)
    level_in = [
        net.send(near_half.at[part_of(zz)], arl.at[k], {"dp": yh * NZ + zz})
        for k, zz in enumerate(level)
    ]
    query_gradient()
    total = near_half[part_of(z), :].astype(F32)
    for k, copy in enumerate(level_in):
        copy.wait_recv()
        total += arl[k].astype(F32)
    net.reuse(KEYS)
    own_rows = half_of(yh, z, ZF)
    agz[own_rows, :] = total.astype(BF)
    level_out = [
        net.send(agz.at[own_rows], agz.at[own_rows], {"dp": yh * NZ + zz}, KEYS) for zz in level
    ]
    total = arflat[part_of(d), :].astype(F32)
    for k, copy in enumerate(sums_in):
        copy.wait_recv()
        total += arz[k].astype(F32)
    agz[part_of(d), :] = total.astype(BF)
    net.reuse(RING)
    sums_out = [
        net.send(agz.at[part_of(d)], agz.at[part_of(d)], {"dp": dd}, RING) for dd in sequences
    ]
    for copy in level_out:
        copy.wait_recv()
    sums_out.append(net.send(agz.at[half_of(yh)], agz.at[half_of(yh)], opposite, KEYS))
    rows_to_heads()
    done = pltpu.make_async_copy(qg_ref, qg_out, local_sems.at[8])
    done.start()
    for copy in sums_out:
        copy.wait_recv()
    done.wait()
    net.finish()
    assert ONCE + net.next[ONCE] == N_SEMS


def hand_over(qg_in, flat, qg_out, wg_ref):
    i = pl.program_id(0)
    n = DSH // 2
    for j in range(LT):
        rows = pl.ds(pl.multiple_of(DSH * j + n * i, 32), n)
        wg_ref[:, 128 * j : 128 * j + 128] = flat[rows, :].astype(F32)
    rope = flat[pl.ds(DSH * LT, n), :].astype(F32)
    wg_ref[:, LAT:] = jnp.where(i == 0, rope[:, :ROPE], rope[:, ROPE:])
    qg_out[...] = qg_in[...]


def on_device(hidden_in, proj_weight, proj_delta, norm_gain, queries, out_grad, seg_map):
    vmem = pl.BlockSpec(memory_space=pltpu.VMEM)
    freqs = np.float32(ROPE_BASE) ** (-(np.arange(HALF, dtype=np.float32) * 2 / ROPE))
    v = pltpu.VMEM
    scratch = [
        pltpu.SMEM((1, 16), jnp.int32), v((DSH, KD), BF), v((DSH, KD), BF), v((1, LAT), F32),
        v((1, HALF), F32),
        v((NQ, H * KD), BF), v((NQ, H * LAT), BF), v((QR, KD), BF), v((QR, LAT), BF),
        v((ROWS, D), BF), v((2 * ROWS, 8 * 512), BF), v((ROWS, 8 * 512), BF), v((8, WF, 128), BF),
        v((2 * ROWS, KD), F32), v((ROWS, KD), F32), v((ROWS, LAT), F32), v((ROWS, 128), F32),
        v((ROWS, ROPE), F32),
        v((16, KF, 128), BF), v((2048, KD), BF), v((2048, QR), F32), v((2048, QR), F32),
        v((2048, QR), BF), v((2048, QR), BF), v((1, QR), F32), v((1, QR), F32),
        v((8, 1, QR), F32), v((1, QR), F32),
        v((8, 2, KF, 128), F32), v((8, 2, KF, 128), BF), v((8, KF, 128), BF), v((QR, KD), F32),
        v((4, 320, 128), BF), v((4, 320, 128), BF),
        v((2, 2, 128, 128), BF), v((2, 2, 128, 128), BF),
        v((2, 2, 256, 128), BF), v((2, 2, 256, 128), BF),
        v((256, 128), BF), v((256, 128), BF),
        v((2, 160, 128), BF), v((2, 160, 128), BF),
        v((2, 320, 128), BF), v((2, 320, 128), BF),
        v((4, 320, 128), F32),
        v((16, KF, 128), BF), v((1024, KD), BF),
        v((8, ROWS, CHIP), BF), v((CHIP, 1024), BF), v((CHIP, KD), F32),
        v((WF, 128), BF), v((WF, 128), BF),
        v((32 * ZF, 128), BF), v((15, ZF, 128), BF), v((7, ZF, 128), BF), v((8 * ZF, 128), BF),
        v((8 * ZF, 128), BF), v((NQ, H * KD), BF),
        pltpu.SemaphoreType.DMA((N_SEMS,)), pltpu.SemaphoreType.DMA((N_SEMS,)),
        pltpu.SemaphoreType.DMA((9,)),
    ]
    query_grad, flat = pl.pallas_call(
        kernel,
        out_shape=(
            jax.ShapeDtypeStruct((NQ, H * KD), BF),
            jax.ShapeDtypeStruct((32 * ZF, 128), BF),
        ),
        in_specs=[pl.BlockSpec(memory_space=pl.ANY)] * 8,
        out_specs=(pl.BlockSpec(memory_space=pl.ANY), vmem),
        scratch_shapes=scratch,
        compiler_params=pltpu.CompilerParams(
            collective_id=0, has_side_effects=True, vmem_limit_bytes=60 * 2**20
        ),
        name="mla_backward",
    )(
        seg_map,
        hidden_in[0],
        proj_weight,
        proj_delta,
        norm_gain.reshape(1, LAT),
        jnp.asarray(freqs.astype(np.float32).reshape(1, HALF)),
        queries[0],
        out_grad[0],
    )
    query_grad, weight_grad = pl.pallas_call(
        hand_over,
        out_shape=(
            jax.ShapeDtypeStruct((NQ, H * KD), BF),
            jax.ShapeDtypeStruct((DSH, KD), F32),
        ),
        grid=(2,),
        in_specs=[
            pl.BlockSpec((NQ, H * KD // 2), lambda i: (0, i)),
            pl.BlockSpec((32 * ZF, 128), lambda i: (0, 0)),
        ],
        out_specs=(
            pl.BlockSpec((NQ, H * KD // 2), lambda i: (0, i)),
            pl.BlockSpec((DSH // 2, KD), lambda i: (i, 0)),
        ),
        name="hand_over",
    )(query_grad, flat)
    return query_grad.reshape(1, NQ, H * KD), weight_grad


def solution(mesh):
    placed = (
        P("dp", "ctx", None),
        P("ctx", None),
        P("ctx", None),
        P(),
        P("dp", "ctx", None),
        P("dp", "ctx", None),
        P("dp", None),
    )
    return jax.shard_map(
        on_device,
        mesh=mesh,
        in_specs=placed,
        out_specs=(P("dp", "ctx", None), P("ctx", None)),
        check_vma=False,
    )
```
